256 devices in a mesh: dp: 8 (over x, core), context: 32 (over z, y).
Axes of the slice: x: 4, y: 4, z: 8, core: 2. Of those that a mesh axis runs over, the one named last changes fastest.
Arguments:
- queries: bfloat16 [8, 4096, 4096], P('dp', 'context'), may hold values from -75 to 75
- keys: bfloat16 [8, 4096, 512], P('dp', 'context'), may hold values from -75 to 75
- values: bfloat16 [8, 4096, 512], P('dp', 'context'), may hold values from -6 to 6
- prefix_cached_keys: bfloat16 [8, 512, 512], P('dp', 'context'), may hold values from -27 to 27
- prefix_cached_values: bfloat16 [8, 512, 512], P('dp', 'context'), may hold values from -6 to 6
- out_grad: bfloat16 [8, 4096, 4096], P('dp', 'context'), may hold values from -6 to 6
- query_gain: float32 [128], replicated, may hold values from 0.6 to 4.5
- key_gain: float32 [128], replicated, may hold values from 0.6 to 4.5
- lengths: int32 [8, 8], P('dp'), may hold values from 1 to 1024, 4096 in all within a row
- offsets: int32 [8, 8], P('dp'), may hold values from 1 to 128, 512 in all within a row
Outputs:
- attention: bfloat16 [8, 4096, 4096], P('dp', 'context')
- query_grad: bfloat16 [8, 4096, 4096], P('dp', 'context')
- key_grad: bfloat16 [8, 4096, 512], P('dp', 'context')
- value_grad: bfloat16 [8, 4096, 512], P('dp', 'context')
- gain_grads: float32 [2, 128], replicated
The draws below stay inside these ranges and needn't reach their ends.
Inputs may be any that keep to these rules, and one draw needn't show every extreme that they name: `lengths`: row g splits window g into 8 pieces laid end to end in order; they sum to 4096, and the longest is exactly 1024. `offsets`: row g holds the cached prefix lengths of the 8 documents of window g, laid end to end in order in its cached rows; they sum to 512, and the longest is exactly 128.
All inputs are finite; a program needn't handle non-finite values.
Results may differ from the reference program's by a relative error of at most 0.017.
The reference program's roundings to bfloat16 on the way count: a program that leaves them out, or rounds other values in their place, can miss the bound.
Values may be sent and summed in bfloat16 or wider, within the bound.
A program may use at most 128 MiB of HBM per device.

```python
import math
import jax
import jax.numpy as jnp
import numpy as np
from jax import lax

HEAD_DIMENSION = 128
QUERY_HEAD_COUNT = 32
KEY_VALUE_HEADS = 4
SEGS = 8
WINDOW_TOKENS = 4096
CACHED_PREFIX = 512
QUERY_WINDOWS = 8
N_CONTEXT = 32


def projected_inputs(key, heads):
    normalized_rows = jnp.clip(jax.random.normal(key, (QUERY_WINDOWS, WINDOW_TOKENS, heads, HEAD_DIMENSION), jnp.float32), -6.0, 6.0)
    return normalized_rows.reshape(QUERY_WINDOWS, WINDOW_TOKENS, heads * HEAD_DIMENSION)


def draw_queries(key, part):
    key = jax.random.fold_in(key, 11)
    return projected_inputs(key, QUERY_HEAD_COUNT).astype(jnp.bfloat16)


def draw_keys(key, part):
    key = jax.random.fold_in(key, 12)
    return projected_inputs(key, KEY_VALUE_HEADS).astype(jnp.bfloat16)


def gain_values(key, lower, upper):
    return jnp.exp(jax.random.uniform(key, (HEAD_DIMENSION,), jnp.float32, math.log(lower), math.log(upper)))


def draw_query_gain(key, part):
    key = jax.random.fold_in(key, 21)
    return gain_values(key, 0.6, 2.0)


def draw_key_gain(key, part):
    key = jax.random.fold_in(key, 22)
    return gain_values(key, 0.6, 2.0)


def draw_prefix_cached_keys(key, part):
    scale_factor = draw_key_gain(key, part)
    key = jax.random.fold_in(key, 31)
    normalized_rows = jnp.clip(jax.random.normal(key, (QUERY_WINDOWS, CACHED_PREFIX, KEY_VALUE_HEADS, HEAD_DIMENSION), jnp.float32), -6.0, 6.0)
    return (normalized_rows * scale_factor[None, None, None, :]).reshape(QUERY_WINDOWS, CACHED_PREFIX, KEY_VALUE_HEADS * HEAD_DIMENSION).astype(jnp.bfloat16)


def levels(own_key, dims, split, smallest, largest):
    gain, own = 1.0, jax.random.fold_in(own_key, 6)
    for dim, parts in split:
        heights = jnp.exp(jax.random.uniform(jax.random.fold_in(own, dim), (parts,), jnp.float32, smallest / len(split), largest / len(split)))
        gain = gain * jnp.repeat(heights, dims[dim] // parts).reshape([-1 if axis == dim else 1 for axis in range(len(dims))])
    return gain


def length_profile(amount, total, bound, skew):
    weights = [(1 << 20) // math.isqrt(rank ** skew) + 1 for rank in range(2, amount + 1)]
    spare, given = total - bound - (amount - 1), [1] * (amount - 1)
    while spare > 0:
        candidates = [i for i in range(amount - 1) if given[i] < bound]
        pool, remaining = sum([weights[i] for i in candidates]), spare
        for i in candidates:
            more = min(bound - given[i], max(1, remaining * weights[i] // pool), spare)
            given[i] = given[i] + more
            spare = spare - more
    return np.array([bound] + given)


def uneven_parts(rng, number_of, total, limit, lean):
    if number_of == 2:
        one = jax.random.randint(rng, (), max(1, total - limit), min(limit, total - 1) + 1)
        return jnp.stack([one, total - one])
    tallies = jnp.asarray(length_profile(number_of, total, limit, lean), jnp.int32)
    twos = (number_of - 1) // 2
    source_of, taker = tallies[1:1 + 2 * twos:2], tallies[2:2 + 2 * twos:2]
    margin = jnp.minimum(source_of - 1, limit - taker)
    passed = jax.random.randint(jax.random.fold_in(rng, 1), (twos,), 0, 1 << 20) % (margin + 1)
    tallies = tallies.at[1:1 + 2 * twos:2].set(source_of - passed).at[2:2 + 2 * twos:2].set(taker + passed)
    return tallies[jax.random.permutation(jax.random.fold_in(rng, 2), number_of)]


def noise(key, extent, width, bound, cuts=(), kind=jnp.bfloat16):
    values = width * jax.random.normal(key, extent, jnp.float32)
    if cuts:
        values = values * levels(key, extent, cuts, -0.22, 0.18)
    return jnp.clip(values, -bound, bound).astype(kind)


def setup_inputs(seed: int = 0) -> dict:
    arg_keys = jax.random.split(jax.random.key(seed), 11)
    return {
        "queries": draw_queries(jax.random.fold_in(arg_keys[10], 71), 0),
        "keys": draw_keys(jax.random.fold_in(arg_keys[10], 71), 0),
        "values": noise(arg_keys[2], (QUERY_WINDOWS, WINDOW_TOKENS, KEY_VALUE_HEADS * HEAD_DIMENSION), 1.0, 6.0, ((0, 8), (1, 32))),
        "prefix_cached_keys": draw_prefix_cached_keys(jax.random.fold_in(arg_keys[10], 71), 0),
        "prefix_cached_values": noise(arg_keys[4], (QUERY_WINDOWS, CACHED_PREFIX, KEY_VALUE_HEADS * HEAD_DIMENSION), 1.0, 6.0, ((0, 8), (1, 32))),
        "out_grad": noise(arg_keys[5], (QUERY_WINDOWS, WINDOW_TOKENS, QUERY_HEAD_COUNT * HEAD_DIMENSION), 1.0, 6.0, ((0, 8), (1, 32))),
        "query_gain": draw_query_gain(jax.random.fold_in(arg_keys[10], 71), 0),
        "key_gain": draw_key_gain(jax.random.fold_in(arg_keys[10], 71), 0),
        "lengths": jax.vmap(lambda own: uneven_parts(own, SEGS, WINDOW_TOKENS, WINDOW_TOKENS // 4, 2))(jax.random.split(arg_keys[8], QUERY_WINDOWS)).reshape((QUERY_WINDOWS, SEGS)).astype(jnp.int32),
        "offsets": jax.vmap(lambda own: uneven_parts(own, SEGS, CACHED_PREFIX, CACHED_PREFIX // 4, 1))(jax.random.split(arg_keys[9], QUERY_WINDOWS)).reshape((QUERY_WINDOWS, SEGS)).astype(jnp.int32),
    }


EPSILON = 1e-06
ROPE_BASE = 1000000.0

def piece_layout(piece_lengths, prefix_lengths, length_total):
    piece_ends = jnp.cumsum(piece_lengths).astype(jnp.int32)
    piece_starts = (piece_ends - piece_lengths).astype(jnp.int32)
    token_index = jnp.arange(length_total, dtype=jnp.int32)
    pieces = lax.optimization_barrier(jnp.sum((token_index[:, None] >= piece_ends[None, :]).astype(jnp.int32), axis=1)).astype(jnp.int32)
    one_hot = (pieces[:, None] == jnp.arange(piece_lengths.shape[0], dtype=jnp.int32)[None, :]).astype(jnp.int32)
    piece_first = lax.optimization_barrier(jnp.sum(one_hot * piece_starts[None, :], axis=1)).astype(jnp.int32)
    prefix_rows = lax.optimization_barrier(jnp.sum(one_hot * prefix_lengths[None, :], axis=1)).astype(jnp.int32)
    positions = (prefix_rows + token_index - piece_first).astype(jnp.int32)
    return (pieces, positions)

def cache_pieces(prefix_lengths, length_total):
    piece_ends = jnp.cumsum(prefix_lengths).astype(jnp.int32)
    token_index = jnp.arange(length_total, dtype=jnp.int32)
    return lax.optimization_barrier(jnp.sum((token_index[:, None] >= piece_ends[None, :]).astype(jnp.int32), axis=1)).astype(jnp.int32)

def rotate_normed(projected, scale_factor, positions):
    head_width = projected.shape[-1]
    half_width = head_width // 2
    normed = projected * lax.rsqrt(lax.optimization_barrier(jnp.mean(projected * projected, axis=-1, keepdims=True)) + EPSILON) * scale_factor
    frequency = jnp.exp(jnp.arange(half_width, dtype=jnp.float32) * (-2.0 * math.log(ROPE_BASE) / head_width))
    angles = positions.astype(jnp.float32)[:, None] * frequency[None, :]
    cosine = jnp.cos(angles)[:, None, :]
    sine_part = jnp.sin(angles)[:, None, :]
    first_half = normed[..., :half_width]
    second_half = normed[..., half_width:]
    return jnp.concatenate([first_half * cosine - second_half * sine_part, second_half * cosine + first_half * sine_part], axis=-1)

def reference(queries, keys, values, prefix_cached_keys, prefix_cached_values, out_grad, query_gain, key_gain, lengths, offsets):
    score_scale = 1.0 / math.sqrt(HEAD_DIMENSION)
    heads_per_group = QUERY_HEAD_COUNT // KEY_VALUE_HEADS
    per_device = QUERY_HEAD_COUNT // N_CONTEXT
    head_replicas = N_CONTEXT // KEY_VALUE_HEADS
    token_index = jnp.arange(WINDOW_TOKENS, dtype=jnp.int32)
    causal = token_index[None, :] <= token_index[:, None]
    attention_list, query_list, key_collection, value_collection = ([], [], [], [])
    query_gain_sum = jnp.zeros((HEAD_DIMENSION,), jnp.float32)
    key_gain_sum = jnp.zeros((HEAD_DIMENSION,), jnp.float32)
    for window_position in range(QUERY_WINDOWS):
        pieces, positions = piece_layout(lengths[window_position], offsets[window_position], WINDOW_TOKENS)
        cached = cache_pieces(offsets[window_position], CACHED_PREFIX)
        allowed = jnp.concatenate([cached[None, :] == pieces[:, None], (pieces[None, :] == pieces[:, None]) & causal], axis=1)
        query_pre = queries[window_position].astype(jnp.float32).reshape(WINDOW_TOKENS, QUERY_HEAD_COUNT, HEAD_DIMENSION)
        query_full, query_pull = jax.vjp(lambda tensor, scale_factor: rotate_normed(tensor, scale_factor, positions), query_pre, query_gain)
        query_rot = query_full.astype(jnp.bfloat16)
        key_before_norm = keys[window_position].astype(jnp.float32).reshape(WINDOW_TOKENS, KEY_VALUE_HEADS, HEAD_DIMENSION)
        key_full, key_pull = jax.vjp(lambda tensor, scale_factor: rotate_normed(tensor, scale_factor, positions), key_before_norm, key_gain)
        key_rotated = key_full.astype(jnp.bfloat16)
        key_row_block = jnp.concatenate([prefix_cached_keys[window_position].reshape(CACHED_PREFIX, KEY_VALUE_HEADS, HEAD_DIMENSION), key_rotated], axis=0)
        value_row_block = jnp.concatenate([prefix_cached_values[window_position].reshape(CACHED_PREFIX, KEY_VALUE_HEADS, HEAD_DIMENSION), values[window_position].reshape(WINDOW_TOKENS, KEY_VALUE_HEADS, HEAD_DIMENSION)], axis=0)
        grad_rows = out_grad[window_position].reshape(WINDOW_TOKENS, QUERY_HEAD_COUNT, HEAD_DIMENSION)

        def one_head(head_index):
            key_head_index = head_index // heads_per_group
            query_head = lax.dynamic_index_in_dim(query_rot, head_index, 1, keepdims=False)
            grad_head = lax.dynamic_index_in_dim(grad_rows, head_index, 1, keepdims=False)
            key_head = lax.dynamic_index_in_dim(key_row_block, key_head_index, 1, keepdims=False)
            value_head = lax.dynamic_index_in_dim(value_row_block, key_head_index, 1, keepdims=False)
            scores = jnp.dot(query_head, key_head.T, preferred_element_type=jnp.float32) * score_scale
            scores = jnp.where(allowed, scores, -jnp.inf)
            row_max = lax.optimization_barrier(jnp.max(scores, axis=1, keepdims=True))
            weights = jnp.exp(scores - row_max)
            prob_full = weights / lax.optimization_barrier(jnp.sum(weights, axis=1, keepdims=True))
            prob_low = prob_full.astype(jnp.bfloat16)
            attention = jnp.dot(prob_low, value_head, preferred_element_type=jnp.float32).astype(jnp.bfloat16)
            grad_prob = jnp.dot(grad_head, value_head.T, preferred_element_type=jnp.float32)
            grad_score = prob_full * (grad_prob - lax.optimization_barrier(jnp.sum(prob_full * grad_prob, axis=1, keepdims=True)))
            grad_low = grad_score.astype(jnp.bfloat16)
            query_rot_grad = (jnp.dot(grad_low, key_head, preferred_element_type=jnp.float32) * score_scale).astype(jnp.bfloat16)
            key_part = jnp.dot(grad_low[:, CACHED_PREFIX:].T, query_head, preferred_element_type=jnp.float32) * score_scale
            value_part = jnp.dot(prob_low[:, CACHED_PREFIX:].T, grad_head, preferred_element_type=jnp.float32)
            return (attention, query_rot_grad, key_part, value_part)
        attention, query_rot_grad, key_parts, value_parts = lax.map(one_head, jnp.arange(QUERY_HEAD_COUNT, dtype=jnp.int32))
        key_shard = lax.optimization_barrier(jnp.sum(key_parts.reshape(N_CONTEXT, per_device, WINDOW_TOKENS, HEAD_DIMENSION), axis=1))
        key_shard = lax.optimization_barrier(key_shard.astype(jnp.bfloat16)).astype(jnp.float32)
        key_gradient_sum = lax.optimization_barrier(jnp.sum(key_shard.reshape(KEY_VALUE_HEADS, head_replicas, WINDOW_TOKENS, HEAD_DIMENSION), axis=1))
        value_shard = lax.optimization_barrier(jnp.sum(value_parts.reshape(N_CONTEXT, per_device, WINDOW_TOKENS, HEAD_DIMENSION), axis=1))
        value_shard = lax.optimization_barrier(value_shard.astype(jnp.bfloat16)).astype(jnp.float32)
        value_gradient_sum = lax.optimization_barrier(jnp.sum(value_shard.reshape(KEY_VALUE_HEADS, head_replicas, WINDOW_TOKENS, HEAD_DIMENSION), axis=1))
        query_back = jnp.transpose(query_rot_grad.astype(jnp.float32), (1, 0, 2))
        query_pre_grad, query_gain_part = query_pull(query_back)
        key_before_norm_gradient, key_gain_part = key_pull(jnp.transpose(key_gradient_sum, (1, 0, 2)))
        query_gain_sum = query_gain_sum + query_gain_part
        key_gain_sum = key_gain_sum + key_gain_part
        attention_list.append(jnp.transpose(attention, (1, 0, 2)).reshape(WINDOW_TOKENS, QUERY_HEAD_COUNT * HEAD_DIMENSION))
        query_list.append(query_pre_grad.astype(jnp.bfloat16).reshape(WINDOW_TOKENS, QUERY_HEAD_COUNT * HEAD_DIMENSION))
        key_collection.append(key_before_norm_gradient.astype(jnp.bfloat16).reshape(WINDOW_TOKENS, KEY_VALUE_HEADS * HEAD_DIMENSION))
        value_collection.append(jnp.transpose(value_gradient_sum, (1, 0, 2)).astype(jnp.bfloat16).reshape(WINDOW_TOKENS, KEY_VALUE_HEADS * HEAD_DIMENSION))
    gain_grads = jnp.stack([query_gain_sum, key_gain_sum])
    return (jnp.stack(attention_list), jnp.stack(query_list), jnp.stack(key_collection), jnp.stack(value_collection), gain_grads)
```

```python
import functools
import math

import jax
import jax.numpy as jnp
from jax import lax
from jax.experimental import pallas as pl
from jax.experimental.pallas import tpu as pltpu
from jax.sharding import PartitionSpec as P

EPSILON = 1e-06
ROPE_BASE = 1000000.0
D = 128
HALF = D // 2
HQ = 8
NY = 4
NZ = 8
ROWS = 128
SLAB = NY * ROWS
COLS = HQ * D
CACHE = 512
CPART = CACHE // (NY * NZ)
WINDOW = 3 * SLAB
KEYS = CACHE + WINDOW
SEGS = 8
REACH = SLAB * 2 + ROWS
MET = CACHE + REACH
CH = 2
NC = HQ // CH
LANES = CH * D
WIDE = 2 * LANES
TILES = ((0, 512), (512, 512), (1024, 512), (1536, 128))
SCALE = 1.0 / math.sqrt(D)
EXP2_SCALE = SCALE * math.log2(math.e)
MASKED = -1e30
F32 = jnp.float32
BF16 = jnp.bfloat16


def aligned(x, n):
    return x if isinstance(x, int) else pl.multiple_of(x, n)


def place():
    c = lax.axis_index("context")
    return lax.div(c, NY), lax.rem(c, NY)


def remote(src, dst, send, recv, z, y):
    return pltpu.make_async_remote_copy(
        src_ref=src,
        dst_ref=dst,
        send_sem=send,
        recv_sem=recv,
        device_id={"context": z * NY + y},
        device_id_type=pl.DeviceIdType.MESH,
    )


def greet_plane(z, y):
    barrier = pltpu.get_barrier_semaphore()
    for d in range(1, NY):
        pl.semaphore_signal(
            barrier,
            inc=1,
            device_id={"context": z * NY + lax.rem(y + d, NY)},
            device_id_type=pl.DeviceIdType.MESH,
        )
    for d in range(1, NZ):
        pl.semaphore_signal(
            barrier,
            inc=1,
            device_id={"context": lax.rem(z + d, NZ) * NY + y},
            device_id_type=pl.DeviceIdType.MESH,
        )
    return barrier


def rotate(a, b, cos, sin):
    return a * cos - b * sin, b * cos + a * sin


def column(row_ref):
    return jnp.broadcast_to(row_ref[...], (D, D)).T


def norm_forward(xt, gain):
    r = lax.rsqrt(jnp.mean(xt * xt, axis=0, keepdims=True) + EPSILON)
    return xt * r * gain


def norm_backward(xt, gain, dyt, cos, sin):
    r = lax.rsqrt(jnp.mean(xt * xt, axis=0, keepdims=True) + EPSILON)
    xh = xt * r
    d1, d2 = dyt[:HALF], dyt[HALF:]
    dn = jnp.concatenate([d1 * cos + d2 * sin, d2 * cos - d1 * sin], axis=0)
    dxh = dn * gain
    dx = r * (dxh - xh * jnp.mean(dxh * xh, axis=0, keepdims=True))
    return dx, dn * xh


def fetch_pieces(lengths_in, offsets_in, lengths, offsets, sems):
    copies = [
        pltpu.make_async_copy(lengths_in, lengths, sems.at[0]),
        pltpu.make_async_copy(offsets_in, offsets, sems.at[1]),
    ]
    for copy in copies:
        copy.start()
    return copies


def fused_kernel(
    ndp,
    lengths_in,
    offsets_in,
    qgain,
    kgain,
    q,
    g,
    k,
    v,
    pk,
    pv,
    attn_out,
    dq_out,
    kg_out,
    vg_out,
    gains_out,
    qs,
    gs,
    ks,
    vs,
    kt,
    vt,
    kraw,
    kx,
    cos_buf,
    sin_buf,
    gain_buf,
    bias,
    xt,
    qt,
    gt,
    qr,
    gr,
    s_buf,
    gp_buf,
    p_hold,
    ds_hold,
    dk,
    dv,
    gacc,
    oh,
    dqh,
    oa,
    oq,
    okg,
    ovg,
    rk,
    rv,
    dkh,
    dvh,
    kg,
    vg,
    gy,
    gz,
    gx,
    lengths,
    offsets,
    psems,
    ysend,
    yrecv,
    qsend,
    qrecv,
    zsend,
    zrecv,
    nsend,
    nrecv,
    csend,
    crecv,
    osend,
    orecv,
    bsend,
    brecv,
    hsend,
    hrecv,
    gsend,
    grecv,
    local,
    olocal,
):
    z, y = place()
    dp = lax.axis_index("dp")
    pieces = fetch_pieces(lengths_in, offsets_in, lengths, offsets, psems)
    barrier = greet_plane(z, y)
    for d in range(1, ndp):
        pl.semaphore_signal(
            barrier,
            inc=1,
            device_id={"dp": lax.rem(dp + d, ndp)},
            device_id_type=pl.DeviceIdType.MESH,
        )
    after, before = lax.rem(z + 1, NZ), lax.rem(z + NZ - 1, NZ)
    for d in range(1, NY):
        pl.semaphore_signal(
            barrier,
            inc=1,
            device_id={"context": before * NY + lax.rem(y + d, NY)},
            device_id_type=pl.DeviceIdType.MESH,
        )
    pl.semaphore_wait(barrier, NY - 1 + NZ - 1 + ndp - 1 + NY - 1)

    own = CACHE + 2 * SLAB
    crow = z * (NY * CPART)
    hops = (2, 1, 3)

    def parts(head, row):
        one = pl.ds(head * D, D)
        cached = pl.ds(crow + row * CPART, CPART)
        return [
            (k.at[:, one], kraw.at[pl.ds(2 * SLAB + row * ROWS, ROWS), :]),
            (v.at[:, one], vs.at[pl.ds(own + row * ROWS, ROWS), :]),
            (pk.at[:, one], ks.at[cached, :]),
            (pv.at[:, one], vs.at[cached, :]),
        ]

    mine = [
        pltpu.make_async_copy(src, dst, local.at[i])
        for i, (src, dst) in enumerate(parts(y, y))
    ]
    ycopies = {}
    zcopies = {}

    def send(i):
        for d in hops:
            yt = lax.rem(y + d, NY)
            src, dst = parts(yt, y)[i]
            copy = remote(src, dst, ysend.at[i, d - 1], yrecv.at[i, d - 1], z, yt)
            copy.start()
            ycopies[i, d] = copy
        mine[i].start()

    def arrived(i):
        mine[i].wait()
        for d in hops:
            ycopies[i, d].wait_recv()

    def send_after(j):
        buf, top = ((kraw, SLAB), (vs, own - SLAB))[j]
        for d in range(NY):
            yt = lax.rem(y + d, NY)
            copy = remote(
                parts(yt, y)[j][0],
                buf.at[pl.ds(top + y * ROWS, ROWS), :],
                nsend.at[j, d],
                nrecv.at[j, d],
                after,
                yt,
            )
            copy.start()
            zcopies[j, d, "next"] = copy

    for j in range(2):
        send_after(j)
    for i in (2, 3, 0, 1):
        send(i)

    whole = pl.ds(y * COLS, COLS)
    here = pl.ds(y * ROWS, ROWS)
    mine_q = [
        pltpu.make_async_copy(x.at[:, whole], buf.at[here, :], local.at[4 + a])
        for a, (x, buf) in enumerate(((q, qs), (g, gs)))
    ]

    def query_copies(w, d):
        yt = lax.rem(y + d, NY)
        return [
            remote(
                x.at[:, pl.ds(yt * COLS + w * WIDE, WIDE)],
                buf.at[here, pl.ds(w * WIDE, WIDE)],
                qsend.at[a, w, d - 1],
                qrecv.at[a, w, d - 1],
                z,
                yt,
            )
            for a, (x, buf) in enumerate(((q, qs), (g, gs)))
        ]

    def send_queries(ways):
        for w, d in ways:
            for copy in query_copies(w, d):
                copy.start()

    for copy in mine_q:
        copy.start()
    send_queries(((0, 3), (0, 1)))

    for copy in pieces:
        copy.wait()

    def per_token(t):
        first = run = jnp.int32(0)
        low = jnp.zeros_like(t)
        clo = jnp.zeros_like(t)
        chi = jnp.zeros_like(t)
        for s in range(SEGS):
            end = first + lengths[0, s]
            stop = run + offsets[0, s]
            inside = (t >= first) & (t < end)
            low = jnp.where(inside, first, low)
            clo = jnp.where(inside, run, clo)
            chi = jnp.where(inside, stop, chi)
            first, run = end, stop
        return low, clo, chi

    t = (z - 2) * SLAB + lax.broadcasted_iota(jnp.int32, (1, WINDOW), 1)
    low, clo, chi = per_token(t)
    frequency = jnp.exp(
        lax.broadcasted_iota(jnp.int32, (HALF, 1), 0).astype(F32)
        * (-2.0 * math.log(ROPE_BASE) / D)
    )
    angles = frequency * (t - low + chi - clo).astype(F32)

    def forward(j):
        x, top = ((kraw, SLAB), (vs, own - SLAB))[j]
        copy = remote(
            x.at[pl.ds(top, SLAB), :],
            x.at[pl.ds(top - SLAB, SLAB), :],
            zsend.at[j],
            zrecv.at[j],
            after,
            y,
        )
        copy.start()
        zcopies[j, "far"] = copy

    kgain_col = column(kgain)[:, :1]

    def rotate_keys(slab):
        rows = slice(slab * SLAB, (slab + 1) * SLAB)
        met = slice(CACHE + slab * SLAB, CACHE + (slab + 1) * SLAB)
        x = kraw[rows, :].T.astype(F32)
        xh = x * lax.rsqrt(jnp.mean(x * x, axis=0, keepdims=True) + EPSILON)
        kx[:, rows] = xh
        n = xh * kgain_col
        a, b = rotate(n[:HALF], n[HALF:], cos_buf[:, rows], sin_buf[:, rows])
        rotated = jnp.concatenate([a, b], axis=0).astype(BF16)
        kt[:, met] = rotated
        ks[met, :] = rotated.T

    cos_buf[...] = jnp.cos(angles)
    sin_buf[...] = jnp.sin(angles)
    gain_buf[...] = column(qgain)
    def cached_to(j, i, rows, d):
        part = (ks, vs)[j].at[rows, :]
        zt = lax.rem(z + d, NZ)
        copy = remote(part, part, csend.at[j, i], crecv.at[j, i], zt, y)
        copy.start()
        zcopies[j, i, "cached"] = copy

    for j in range(2):
        arrived(2 + j)
        for i, d in enumerate((1, 2, 5, 6, 7)):
            cached_to(j, i, pl.ds(crow, NY * CPART), d)
    for j in range(2):
        for d in range(NY):
            zcopies[j, d, "next"].wait_recv()
        forward(j)
    send_queries(((1, 3), (1, 1), (0, 2), (1, 2)))

    def mask(b, carry):
        t = z * SLAB + b * ROWS + lax.broadcasted_iota(jnp.int32, (1, ROWS), 1)
        low, clo, chi = per_token(t)
        rows = lax.broadcasted_iota(jnp.int32, (CACHE, ROWS), 0)
        base = aligned(b * MET, ROWS)
        seen = (rows >= clo) & (rows < chi)
        bias[pl.ds(base, CACHE), :] = jnp.where(seen, 0.0, MASKED)
        rows = lax.broadcasted_iota(jnp.int32, (REACH, ROWS), 0)
        token = rows + ((z - 2) * SLAB + b * ROWS)
        seen = (token >= low) & (token <= t)
        base = aligned(b * MET + CACHE, ROWS)
        bias[pl.ds(base, REACH), :] = jnp.where(seen, 0.0, MASKED)
        return carry

    lax.fori_loop(0, NY, mask, 0)
    dk[...] = jnp.zeros_like(dk)
    dv[...] = jnp.zeros_like(dv)
    gacc[...] = jnp.zeros_like(gacc)

    arrived(0)
    rotate_keys(2)
    arrived(1)
    vt[:, own:] = vs[own:, :].T
    for j in range(2):
        zcopies[j, 2, "cached"].wait_recv()
        for i, d in ((5, 7), (6, 6)):
            cached_to(j, i, pl.ds(lax.rem(z + 3, NZ) * (NY * CPART), NY * CPART), d)
    rotate_keys(1)
    vt[:, CACHE + SLAB : own] = vs[CACHE + SLAB : own, :].T

    def spot(w, b, u=0):
        return aligned((w * NY + b) * WIDE + u * LANES, LANES)

    def prepare(w, b):
        rows = pl.ds(aligned(b * ROWS, ROWS), ROWS)
        now = pl.ds(aligned(2 * SLAB + b * ROWS, ROWS), ROWS)
        cos = cos_buf[:, now]
        sin = sin_buf[:, now]
        for h in range(2 * CH):
            cols = pl.ds(aligned(w * WIDE + h * D, D), D)
            lanes = pl.ds(aligned(spot(w, b) + h * D, D), D)
            x = qs[rows, cols].T
            xt[:, lanes] = x
            n = norm_forward(x.astype(F32), gain_buf[...])
            r1, r2 = rotate(n[:HALF], n[HALF:], cos, sin)
            rot = jnp.concatenate([r1, r2], axis=0).astype(BF16)
            qt[:, lanes] = rot
            qr[lanes, :] = rot.T
            grad = gs[rows, cols]
            gr[lanes, :] = grad
            gt[:, lanes] = grad.T

    for copy in mine_q:
        copy.wait()

    for j, (x, xtr) in enumerate(((ks, kt), (vs, vt))):
        for i in range(NZ - 1):
            if i != 2:
                zcopies[j, i, "cached"].wait_recv()
        xtr[:, :CACHE] = x[:CACHE, :].T
    zcopies[0, "far"].wait_recv()
    rotate_keys(0)
    zcopies[1, "far"].wait_recv()
    vt[:, CACHE : CACHE + SLAB] = vs[CACHE : CACHE + SLAB, :].T

    def groups(x):
        return x.reshape(x.shape[0] // 8, 8, LANES)

    sides = range(2)

    def tile(b, first, rows):
        if first < CACHE:
            return pl.ds(first, rows)
        return pl.ds(aligned(first + b * ROWS, ROWS), rows)

    def attend(w, b, held=False):
        lanes = [pl.ds(spot(w, b, u), LANES) for u in sides]
        unit_lanes = pl.ds(spot(w, b), WIDE)

        top = [jnp.full((8, LANES), MASKED, F32) for _ in sides]
        for first, n in TILES:
            at = slice(first, first + n)
            add = bias[pl.ds(aligned(b * MET + first, ROWS), n), :]
            add = jnp.concatenate([add] * CH, axis=1)
            kb = ks[tile(b, first, n), :]
            for u in sides:
                sc = jnp.dot(kb, qt[:, lanes[u]], preferred_element_type=F32)
                sc = sc * EXP2_SCALE + add
                s_buf[u, at, :] = sc
                top[u] = jnp.maximum(top[u], jnp.max(groups(sc), axis=0))
        top = [jnp.max(x, axis=0, keepdims=True) for x in top]
        sums = [jnp.zeros((8, LANES), F32) for _ in sides]
        dots = [jnp.zeros((8, LANES), F32) for _ in sides]
        for first, n in TILES:
            at = slice(first, first + n)
            vb = vs[tile(b, first, n), :]
            for u in sides:
                gp = jnp.dot(vb, gt[:, lanes[u]], preferred_element_type=F32)
                w2 = jnp.exp2(s_buf[u, at, :] - top[u])
                gp_buf[u, at, :] = gp
                sums[u] = sums[u] + jnp.sum(groups(w2), axis=0)
                dots[u] = dots[u] + jnp.sum(groups(w2 * gp), axis=0)
        sums = [jnp.sum(x, axis=0, keepdims=True) for x in sums]
        mean = [jnp.sum(x, axis=0, keepdims=True) / r for x, r in zip(dots, sums)]
        less = [m + jnp.log(x) * math.log2(math.e) for m, x in zip(top, sums)]
        qrow = qr[unit_lanes, :]
        grow = gr[unit_lanes, :]
        ot = [jnp.zeros((D, LANES), F32) for _ in sides]
        dqt = [jnp.zeros((D, LANES), F32) for _ in sides]
        for first, n in TILES:
            at = slice(first, first + n)
            rows = tile(b, first, n)
            probs, grads = [], []
            for u in sides:
                prob = jnp.exp2(s_buf[u, at, :] - less[u])
                ds = (prob * (gp_buf[u, at, :] - mean[u])).astype(BF16)
                prob = prob.astype(BF16)
                if not held:
                    ot[u] += jnp.dot(vt[:, rows], prob, preferred_element_type=F32)
                    dqt[u] += jnp.dot(kt[:, rows], ds, preferred_element_type=F32)
                probs.append(prob)
                grads.append(ds)
            prob = jnp.concatenate(probs, axis=1)
            ds = jnp.concatenate(grads, axis=1)
            if held:
                p_hold[at, :] = prob
                ds_hold[at, :] = ds
            if first >= CACHE:
                dk[rows, :] += jnp.dot(ds, qrow, preferred_element_type=F32)
                dv[rows, :] += jnp.dot(prob, grow, preferred_element_type=F32)
        if not held:
            for u in sides:
                close(w, u, b, ot[u], dqt[u])

    def rest(w, b):
        for u in sides:
            part = slice(u * LANES, (u + 1) * LANES)
            ot = jnp.zeros((D, LANES), F32)
            dqt = jnp.zeros((D, LANES), F32)
            for first, n in TILES:
                at = slice(first, first + n)
                rows = tile(b, first, n)
                ot += jnp.dot(vt[:, rows], p_hold[at, part], preferred_element_type=F32)
                dqt += jnp.dot(kt[:, rows], ds_hold[at, part], preferred_element_type=F32)
            close(w, u, b, ot, dqt)

    def close(w, u, b, ot, dqt):
        here = pl.ds(aligned(b * ROWS, ROWS), ROWS)
        now = pl.ds(aligned(2 * SLAB + b * ROWS, ROWS), ROWS)
        cos = cos_buf[:, now]
        sin = sin_buf[:, now]
        out = ot.astype(BF16)
        back = (dqt * SCALE).astype(BF16).astype(F32)
        for h in range(CH):
            cols = pl.ds(aligned(w * WIDE + u * LANES + h * D, D), D)
            part = slice(h * D, (h + 1) * D)
            oh[here, cols] = out[:, part].T
            x = xt[:, pl.ds(aligned(spot(w, b, u) + h * D, D), D)].astype(F32)
            dx, term = norm_backward(x, gain_buf[...], back[:, part], cos, sin)
            gacc[...] += term
            dqh[here, cols] = dx.astype(BF16).T

    def out_copies(w, d):
        yt = lax.rem(y + d, NY)
        return [
            remote(
                x.at[pl.ds(yt * ROWS, ROWS), pl.ds(w * WIDE, WIDE)],
                buf.at[:, pl.ds(y * COLS + w * WIDE, WIDE)],
                osend.at[a, w, d - 1],
                orecv.at[a, w, d - 1],
                z,
                yt,
            )
            for a, (x, buf) in enumerate(((oh, oa), (dqh, oq)))
        ]

    def out_stays(w):
        return [
            pltpu.make_async_copy(
                x.at[here, pl.ds(w * WIDE, WIDE)],
                buf.at[:, pl.ds(y * COLS + w * WIDE, WIDE)],
                olocal.at[a, w],
            )
            for a, (x, buf) in enumerate(((oh, oa), (dqh, oq)))
        ]

    def step(n, carry):
        w = jnp.where((n == 3) | (n == 4) | (n == 6), 1, 0)
        d = jnp.where(n == 0, 0, jnp.where(n > 4, 2, jnp.where((n == 1) | (n == 3), 1, 3)))
        b = lax.rem(y + d, NY)

        @pl.when(n > 0)
        def _():
            for copy in query_copies(w, NY - d):
                copy.wait_recv()

        prepare(w, b)
        attend(w, b)

        @pl.when(n > 0)
        def _():
            for copy in out_copies(w, d):
                copy.start()

        return carry

    lax.fori_loop(0, 7, step, 0)
    for copy in out_stays(0):
        copy.start()

    half = SLAB // 2
    lower, upper = slice(0, half), slice(half, SLAB)
    sums = ((dk, dkh, rk, SCALE), (dv, dvh, rv, 1.0))

    def back(i, hop, h):
        low, got = sums[i][1], sums[i][2]
        part = pl.ds(h * half, half)
        return remote(
            low.at[h] if hop == 0 else got.at[0, part, :],
            got.at[hop, part, :],
            hsend.at[i, hop, h],
            hrecv.at[i, hop, h],
            before,
            y,
        )

    def first_hop(h):
        for i, (total, low, _, scale) in enumerate(sums):
            rows = slice(CACHE + h * half, CACHE + (h + 1) * half)
            low[h] = (total[rows, :] * scale).astype(BF16)
            back(i, 0, h).start()

    def second_hop(h):
        for i, (total, _, got, scale) in enumerate(sums):
            back(i, 0, h).wait_recv()
            rows = slice(CACHE + SLAB + h * half, CACHE + SLAB + (h + 1) * half)
            at = (lower, upper)[h]
            mid = total[rows, :] * scale + got[0, at, :].astype(F32)
            got[0, at, :] = mid.astype(BF16)
            back(i, 1, h).start()

    prepare(1, y)
    attend(1, y, True)
    first_hop(0)
    first_hop(1)
    rest(1, y)
    for copy in out_stays(1):
        copy.start()
    second_hop(0)

    terms = jnp.zeros((D, ROWS), F32)
    for slab in range(3):
        rows = slice(slab * SLAB, (slab + 1) * SLAB)
        dkt = (dk[CACHE + slab * SLAB : CACHE + (slab + 1) * SLAB, :] * SCALE).T
        a, b = rotate(dkt[:HALF], dkt[HALF:], cos_buf[:, rows], -sin_buf[:, rows])
        term = jnp.concatenate([a, b], axis=0) * kx[:, rows]
        for i in range(SLAB // ROWS):
            terms = terms + term[:, i * ROWS : (i + 1) * ROWS]
    rows = [jnp.sum(x.T, axis=0, keepdims=True) for x in (gacc[...], terms)]
    total = jnp.concatenate(rows + [jnp.zeros((6, D), F32)], axis=0)

    def share(buf, me, n, first, total, device):
        buf[me] = total
        copies = []
        for d in range(1, n):
            copies.append(
                pltpu.make_async_remote_copy(
                    src_ref=buf.at[me],
                    dst_ref=buf.at[me],
                    send_sem=gsend.at[first + d - 1],
                    recv_sem=grecv.at[first + d - 1],
                    device_id=device(lax.rem(me + d, n)),
                    device_id_type=pl.DeviceIdType.MESH,
                )
            )
            copies[-1].start()
        return copies

    def add_up(copies, buf, n):
        for copy in copies:
            copy.wait()
        total = buf[0]
        for i in range(1, n):
            total = total + buf[i]
        return total

    second_hop(1)
    shared = share(gx, dp, ndp, NY + NZ - 2, total, lambda to: {"dp": to})
    kv_out = []

    def leave_row(i, x, buf):
        there = buf.at[:, pl.ds(y * D, D)]
        copies = []
        for d in hops:
            yt = lax.rem(y + d, NY)
            copies.append(
                remote(
                    x.at[pl.ds(yt * ROWS, ROWS), :],
                    there,
                    bsend.at[i, d - 1],
                    brecv.at[i, d - 1],
                    z,
                    yt,
                )
            )
        copies.append(pltpu.make_async_copy(x.at[here, :], there, local.at[i]))
        for copy in copies:
            copy.start()
        kv_out.extend(copies)

    total = add_up(shared, gx, ndp)
    shared = share(gz, z, NZ, NY - 1, total, lambda to: {"context": to * NY + y})
    for h in range(2):
        back(0, 1, h).wait_recv()
        at = (lower, upper)[h]
        rows = slice(own + h * half, own + (h + 1) * half)
        raw = slice(2 * SLAB + h * half, 2 * SLAB + (h + 1) * half)
        dkt = (dk[rows, :] * SCALE + rk[1, at, :].astype(F32)).T
        dx, _ = norm_backward(
            kraw[raw, :].T.astype(F32), kgain_col, dkt, cos_buf[:, raw], sin_buf[:, raw]
        )
        kg[at, :] = dx.astype(BF16).T
    leave_row(0, kg, okg)
    total = add_up(shared, gz, NZ)
    shared = share(gy, y, NY, 0, total, lambda to: {"context": z * NY + to})
    for h in range(2):
        back(1, 1, h).wait_recv()
    vg[...] = (dv[own:, :] + rv[1].astype(F32)).astype(BF16)
    leave_row(1, vg, ovg)
    gains_out[...] = add_up(shared, gy, NY)[:2]

    for w in range(2):
        for d in hops:
            for copy in out_copies(w, d):
                copy.wait()
            for copy in query_copies(w, d):
                copy.wait_send()
        for copy in out_stays(w):
            copy.wait()
    leaving = [
        pltpu.make_async_copy(oa, attn_out, local.at[2]),
        pltpu.make_async_copy(oq, dq_out, local.at[3]),
    ]
    for copy in leaving:
        copy.start()
    for copy in kv_out:
        copy.wait()
    for i, (x, out) in enumerate(((okg, kg_out), (ovg, vg_out))):
        copy = pltpu.make_async_copy(x, out, local.at[4 + i])
        copy.start()
        leaving.append(copy)
    for copies in (ycopies, zcopies):
        for copy in copies.values():
            copy.wait_send()
    for i in range(2):
        for hop in range(2):
            for h in range(2):
                back(i, hop, h).wait_send()
    for copy in leaving:
        copy.wait()


def finish_kernel(*refs):
    n = (len(refs) - 1) // 3
    sems = refs[-1]
    into = [
        pltpu.make_async_copy(refs[i], refs[2 * n + i], sems.at[0, i]) for i in range(n)
    ]
    out = [
        pltpu.make_async_copy(refs[2 * n + i], refs[n + i], sems.at[1, i])
        for i in range(n)
    ]
    for copy in into:
        copy.start()
    for a, b in zip(into, out):
        a.wait()
        b.start()
    for copy in out:
        copy.wait()


VMEM = pl.BlockSpec(memory_space=pltpu.VMEM)
HBM = pl.BlockSpec(memory_space=pltpu.HBM)
ANY = pl.BlockSpec(memory_space=pl.ANY)
DMA = pltpu.SemaphoreType.DMA


def body(queries, keys, values, pkeys, pvalues, out_grad, query_gain, key_gain, lengths, offsets):
    ndp = lax.axis_size("dp")
    sd = jax.ShapeDtypeStruct

    def vmem(shape, dtype, count=1):
        return [pltpu.VMEM(shape, dtype)] * count

    def dma(shape, count=2):
        return [DMA(shape)] * count

    results = pl.pallas_call(
        functools.partial(fused_kernel, ndp),
        name="fused",
        out_shape=(
            sd((ROWS, NY * COLS), BF16),
            sd((ROWS, NY * COLS), BF16),
            sd((ROWS, NY * D), BF16),
            sd((ROWS, NY * D), BF16),
            sd((2, D), F32),
        ),
        in_specs=[HBM] * 2 + [VMEM] * 2 + [HBM] * 6,
        out_specs=(ANY, ANY, ANY, ANY, VMEM),
        scratch_shapes=vmem((SLAB, COLS), BF16, 2)
        + vmem((KEYS, D), BF16, 2)
        + vmem((D, KEYS), BF16, 2)
        + vmem((WINDOW, D), BF16)
        + vmem((D, WINDOW), F32)
        + vmem((HALF, WINDOW), F32, 2)
        + vmem((D, D), F32)
        + vmem((NY * MET, ROWS), F32)
        + vmem((D, HQ * SLAB), BF16, 3)
        + vmem((HQ * SLAB, D), BF16, 2)
        + vmem((2, MET, LANES), F32, 2)
        + vmem((MET, WIDE), BF16, 2)
        + vmem((KEYS, D), F32, 2)
        + vmem((D, ROWS), F32)
        + vmem((SLAB, COLS), BF16, 2)
        + vmem((ROWS, NY * COLS), BF16, 2)
        + vmem((ROWS, NY * D), BF16, 2)
        + vmem((2, SLAB, D), BF16, 2)
        + vmem((2, SLAB // 2, D), BF16, 2)
        + vmem((SLAB, D), BF16, 2)
        + vmem((NY, 8, D), F32)
        + vmem((NZ, 8, D), F32)
        + vmem((ndp, 8, D), F32)
        + [pltpu.SMEM((1, SEGS), jnp.int32)] * 2
        + dma((2,), 1)
        + dma((4, NY - 1))
        + dma((2, 2, NY - 1))
        + dma((2,))
        + dma((2, NY))
        + dma((2, NZ - 1))
        + dma((2, 2, NY - 1))
        + dma((2, NY - 1))
        + dma((2, 2, 2))
        + dma((NY + NZ + ndp - 3,))
        + dma((6,), 1)
        + dma((2, 2), 1),
        compiler_params=pltpu.CompilerParams(
            collective_id=0, has_side_effects=True, vmem_limit_bytes=62 << 20
        ),
    )(
        lengths,
        offsets,
        query_gain.reshape(1, D),
        key_gain.reshape(1, D),
        queries[0],
        out_grad[0],
        keys[0],
        values[0],
        pkeys[0],
        pvalues[0],
    )
    attention, query_grad, key_grad, value_grad, gains = pl.pallas_call(
        finish_kernel,
        name="finish",
        out_shape=[sd(x.shape, x.dtype) for x in results],
        in_specs=[ANY] * 5,
        out_specs=[HBM] * 5,
        scratch_shapes=[pltpu.VMEM(x.shape, x.dtype) for x in results] + [DMA((2, 5))],
        compiler_params=pltpu.CompilerParams(vmem_limit_bytes=62 << 20),
    )(*results)
    return attention[None], query_grad[None], key_grad[None], value_grad[None], gains


def solution(mesh):
    rows = P("dp", "context", None)
    in_specs = (rows,) * 6 + (P(), P(), P("dp", None), P("dp", None))
    out_specs = (rows,) * 4 + (P(),)
    return jax.shard_map(body, mesh=mesh, in_specs=in_specs, out_specs=out_specs, check_vma=False)
```

```python
import functools
import math

import jax
import jax.numpy as jnp
from jax import lax
from jax.experimental import pallas as pl
from jax.experimental.pallas import tpu as pltpu
from jax.sharding import PartitionSpec as P

EPSILON = 1e-06
ROPE_BASE = 1000000.0
D = 128
HALF = D // 2
HQ = 8
NY = 4
NZ = 8
ROWS = 128
SLAB = NY * ROWS
COLS = HQ * D
CACHE = 512
CPART = CACHE // (NY * NZ)
WINDOW = 3 * SLAB
KEYS = CACHE + WINDOW
SEGS = 8
REACH = SLAB * 2 + ROWS
MET = CACHE + REACH
CH = 2
NC = HQ // CH
LANES = CH * D
WIDE = 2 * LANES
TILES = ((0, 512), (512, 512), (1024, 512), (1536, 128))
SCALE = 1.0 / math.sqrt(D)
EXP2_SCALE = SCALE * math.log2(math.e)
MASKED = -1e30
F32 = jnp.float32
BF16 = jnp.bfloat16


def aligned(x, n):
    return x if isinstance(x, int) else pl.multiple_of(x, n)


def place():
    c = lax.axis_index("context")
    return lax.div(c, NY), lax.rem(c, NY)


def remote(src, dst, send, recv, z, y):
    return pltpu.make_async_remote_copy(
        src_ref=src,
        dst_ref=dst,
        send_sem=send,
        recv_sem=recv,
        device_id={"context": z * NY + y},
        device_id_type=pl.DeviceIdType.MESH,
    )


def greet_plane(z, y):
    barrier = pltpu.get_barrier_semaphore()
    for d in range(1, NY):
        pl.semaphore_signal(
            barrier,
            inc=1,
            device_id={"context": z * NY + lax.rem(y + d, NY)},
            device_id_type=pl.DeviceIdType.MESH,
        )
    for d in range(1, NZ):
        pl.semaphore_signal(
            barrier,
            inc=1,
            device_id={"context": lax.rem(z + d, NZ) * NY + y},
            device_id_type=pl.DeviceIdType.MESH,
        )
    return barrier


def rotate(a, b, cos, sin):
    return a * cos - b * sin, b * cos + a * sin


def column(row_ref):
    return jnp.broadcast_to(row_ref[...], (D, D)).T


def norm_forward(xt, gain):
    r = lax.rsqrt(jnp.mean(xt * xt, axis=0, keepdims=True) + EPSILON)
    return xt * r * gain


def norm_backward(xt, gain, dyt, cos, sin):
    r = lax.rsqrt(jnp.mean(xt * xt, axis=0, keepdims=True) + EPSILON)
    xh = xt * r
    d1, d2 = dyt[:HALF], dyt[HALF:]
    dn = jnp.concatenate([d1 * cos + d2 * sin, d2 * cos - d1 * sin], axis=0)
    dxh = dn * gain
    dx = r * (dxh - xh * jnp.mean(dxh * xh, axis=0, keepdims=True))
    return dx, dn * xh


def fetch_pieces(lengths_in, offsets_in, lengths, offsets, sems):
    copies = [
        pltpu.make_async_copy(lengths_in, lengths, sems.at[0]),
        pltpu.make_async_copy(offsets_in, offsets, sems.at[1]),
    ]
    for copy in copies:
        copy.start()
    return copies


def fused_kernel(
    ndp,
    lengths_in,
    offsets_in,
    qgain,
    kgain,
    q,
    g,
    k,
    v,
    pk,
    pv,
    attn_out,
    dq_out,
    kg_out,
    vg_out,
    gains_out,
    qs,
    gs,
    ks,
    vs,
    kt,
    vt,
    kraw,
    kx,
    cos_buf,
    sin_buf,
    gain_buf,
    bias,
    xt,
    qt,
    gt,
    qr,
    gr,
    s_buf,
    gp_buf,
    p_hold,
    ds_hold,
    dk,
    dv,
    gacc,
    oh,
    dqh,
    oa,
    oq,
    okg,
    ovg,
    rk,
    rv,
    dkh,
    dvh,
    kg,
    vg,
    gy,
    gz,
    gx,
    lengths,
    offsets,
    psems,
    ysend,
    yrecv,
    qsend,
    qrecv,
    zsend,
    zrecv,
    nsend,
    nrecv,
    csend,
    crecv,
    osend,
    orecv,
    bsend,
    brecv,
    hsend,
    hrecv,
    gsend,
    grecv,
    local,
    olocal,
):
    z, y = place()
    dp = lax.axis_index("dp")
    pieces = fetch_pieces(lengths_in, offsets_in, lengths, offsets, psems)
    barrier = greet_plane(z, y)
    for d in range(1, ndp):
        pl.semaphore_signal(
            barrier,
            inc=1,
            device_id={"dp": lax.rem(dp + d, ndp)},
            device_id_type=pl.DeviceIdType.MESH,
        )
    after, before = lax.rem(z + 1, NZ), lax.rem(z + NZ - 1, NZ)
    for d in range(1, NY):
        pl.semaphore_signal(
            barrier,
            inc=1,
            device_id={"context": before * NY + lax.rem(y + d, NY)},
            device_id_type=pl.DeviceIdType.MESH,
        )
    pl.semaphore_wait(barrier, NY - 1 + NZ - 1 + ndp - 1 + NY - 1)

    own = CACHE + 2 * SLAB
    crow = z * (NY * CPART)
    hops = (2, 1, 3)

    def parts(head, row):
        one = pl.ds(head * D, D)
        cached = pl.ds(crow + row * CPART, CPART)
        return [
            (k.at[:, one], kraw.at[pl.ds(2 * SLAB + row * ROWS, ROWS), :]),
            (v.at[:, one], vs.at[pl.ds(own + row * ROWS, ROWS), :]),
            (pk.at[:, one], ks.at[cached, :]),
            (pv.at[:, one], vs.at[cached, :]),
        ]

    mine = [
        pltpu.make_async_copy(src, dst, local.at[i])
        for i, (src, dst) in enumerate(parts(y, y))
    ]
    ycopies = {}
    zcopies = {}

    def send(i):
        for d in hops:
            yt = lax.rem(y + d, NY)
            src, dst = parts(yt, y)[i]
            copy = remote(src, dst, ysend.at[i, d - 1], yrecv.at[i, d - 1], z, yt)
            copy.start()
            ycopies[i, d] = copy
        mine[i].start()

    def arrived(i):
        mine[i].wait()
        for d in hops:
            ycopies[i, d].wait_recv()

    def send_after(j):
        buf, top = ((kraw, SLAB), (vs, own - SLAB))[j]
        for d in range(NY):
            yt = lax.rem(y + d, NY)
            copy = remote(
                parts(yt, y)[j][0],
                buf.at[pl.ds(top + y * ROWS, ROWS), :],
                nsend.at[j, d],
                nrecv.at[j, d],
                after,
                yt,
            )
            copy.start()
            zcopies[j, d, "next"] = copy

    for j in range(2):
        send_after(j)
    for i in (2, 3, 0, 1):
        send(i)

    whole = pl.ds(y * COLS, COLS)
    here = pl.ds(y * ROWS, ROWS)
    mine_q = [
        pltpu.make_async_copy(x.at[:, whole], buf.at[here, :], local.at[4 + a])
        for a, (x, buf) in enumerate(((q, qs), (g, gs)))
    ]

    def query_copies(w, d):
        yt = lax.rem(y + d, NY)
        return [
            remote(
                x.at[:, pl.ds(yt * COLS + w * WIDE, WIDE)],
                buf.at[here, pl.ds(w * WIDE, WIDE)],
                qsend.at[a, w, d - 1],
                qrecv.at[a, w, d - 1],
                z,
                yt,
            )
            for a, (x, buf) in enumerate(((q, qs), (g, gs)))
        ]

    def send_queries(ways):
        for w, d in ways:
            for copy in query_copies(w, d):
                copy.start()

    for copy in mine_q:
        copy.start()
    send_queries(((0, 3), (0, 1)))

    for copy in pieces:
        copy.wait()

    def per_token(t):
        first = run = jnp.int32(0)
        low = jnp.zeros_like(t)
        clo = jnp.zeros_like(t)
        chi = jnp.zeros_like(t)
        for s in range(SEGS):
            end = first + lengths[0, s]
            stop = run + offsets[0, s]
            inside = (t >= first) & (t < end)
            low = jnp.where(inside, first, low)
            clo = jnp.where(inside, run, clo)
            chi = jnp.where(inside, stop, chi)
            first, run = end, stop
        return low, clo, chi

    t = (z - 2) * SLAB + lax.broadcasted_iota(jnp.int32, (1, WINDOW), 1)
    low, clo, chi = per_token(t)
    frequency = jnp.exp(
        lax.broadcasted_iota(jnp.int32, (HALF, 1), 0).astype(F32)
        * (-2.0 * math.log(ROPE_BASE) / D)
    )
    angles = frequency * (t - low + chi - clo).astype(F32)

    def forward(j):
        x, top = ((kraw, SLAB), (vs, own - SLAB))[j]
        copy = remote(
            x.at[pl.ds(top, SLAB), :],
            x.at[pl.ds(top - SLAB, SLAB), :],
            zsend.at[j],
            zrecv.at[j],
            after,
            y,
        )
        copy.start()
        zcopies[j, "far"] = copy

    kgain_col = column(kgain)[:, :1]

    def rotate_keys(slab):
        rows = slice(slab * SLAB, (slab + 1) * SLAB)
        met = slice(CACHE + slab * SLAB, CACHE + (slab + 1) * SLAB)
        x = kraw[rows, :].T.astype(F32)
        xh = x * lax.rsqrt(jnp.mean(x * x, axis=0, keepdims=True) + EPSILON)
        kx[:, rows] = xh
        n = xh * kgain_col
        a, b = rotate(n[:HALF], n[HALF:], cos_buf[:, rows], sin_buf[:, rows])
        rotated = jnp.concatenate([a, b], axis=0).astype(BF16)
        kt[:, met] = rotated
        ks[met, :] = rotated.T

    cos_buf[...] = jnp.cos(angles)
    sin_buf[...] = jnp.sin(angles)
    gain_buf[...] = column(qgain)
    def cached_to(j, i, rows, d):
        part = (ks, vs)[j].at[rows, :]
        zt = lax.rem(z + d, NZ)
        copy = remote(part, part, csend.at[j, i], crecv.at[j, i], zt, y)
        copy.start()
        zcopies[j, i, "cached"] = copy

    for j in range(2):
        arrived(2 + j)
        for i, d in enumerate((1, 2, 5, 6, 7)):
            cached_to(j, i, pl.ds(crow, NY * CPART), d)
    for j in range(2):
        for d in range(NY):
            zcopies[j, d, "next"].wait_recv()
        forward(j)
    send_queries(((1, 3), (1, 1), (0, 2), (1, 2)))

    def mask(b, carry):
        t = z * SLAB + b * ROWS + lax.broadcasted_iota(jnp.int32, (1, ROWS), 1)
        low, clo, chi = per_token(t)
        rows = lax.broadcasted_iota(jnp.int32, (CACHE, ROWS), 0)
        base = aligned(b * MET, ROWS)
        seen = (rows >= clo) & (rows < chi)
        bias[pl.ds(base, CACHE), :] = jnp.where(seen, 0.0, MASKED)
        rows = lax.broadcasted_iota(jnp.int32, (REACH, ROWS), 0)
        token = rows + ((z - 2) * SLAB + b * ROWS)
        seen = (token >= low) & (token <= t)
        base = aligned(b * MET + CACHE, ROWS)
        bias[pl.ds(base, REACH), :] = jnp.where(seen, 0.0, MASKED)
        return carry

    lax.fori_loop(0, NY, mask, 0)
    dk[...] = jnp.zeros_like(dk)
    dv[...] = jnp.zeros_like(dv)
    gacc[...] = jnp.zeros_like(gacc)

    arrived(0)
    rotate_keys(2)
    arrived(1)
    vt[:, own:] = vs[own:, :].T
    for j in range(2):
        zcopies[j, 2, "cached"].wait_recv()
        for i, d in ((5, 7), (6, 6)):
            cached_to(j, i, pl.ds(lax.rem(z + 3, NZ) * (NY * CPART), NY * CPART), d)
    rotate_keys(1)
    vt[:, CACHE + SLAB : own] = vs[CACHE + SLAB : own, :].T

    def spot(w, b, u=0):
        return aligned((w * NY + b) * WIDE + u * LANES, LANES)

    def prepare(w, b):
        rows = pl.ds(aligned(b * ROWS, ROWS), ROWS)
        now = pl.ds(aligned(2 * SLAB + b * ROWS, ROWS), ROWS)
        cos = cos_buf[:, now]
        sin = sin_buf[:, now]
        for h in range(2 * CH):
            cols = pl.ds(aligned(w * WIDE + h * D, D), D)
            lanes = pl.ds(aligned(spot(w, b) + h * D, D), D)
            x = qs[rows, cols].T
            xt[:, lanes] = x
            n = norm_forward(x.astype(F32), gain_buf[...])
            r1, r2 = rotate(n[:HALF], n[HALF:], cos, sin)
            rot = jnp.concatenate([r1, r2], axis=0).astype(BF16)
            qt[:, lanes] = rot
            qr[lanes, :] = rot.T
            grad = gs[rows, cols]
            gr[lanes, :] = grad
            gt[:, lanes] = grad.T

    for copy in mine_q:
        copy.wait()

    for j, (x, xtr) in enumerate(((ks, kt), (vs, vt))):
        for i in range(NZ - 1):
            if i != 2:
                zcopies[j, i, "cached"].wait_recv()
        xtr[:, :CACHE] = x[:CACHE, :].T
    prepare(0, y)
    zcopies[0, "far"].wait_recv()
    rotate_keys(0)
    zcopies[1, "far"].wait_recv()
    vt[:, CACHE : CACHE + SLAB] = vs[CACHE : CACHE + SLAB, :].T

    def groups(x):
        return x.reshape(x.shape[0] // 8, 8, LANES)

    sides = range(2)

    def tile(b, first, rows):
        if first < CACHE:
            return pl.ds(first, rows)
        return pl.ds(aligned(first + b * ROWS, ROWS), rows)

    def attend(w, b, held=False):
        lanes = [pl.ds(spot(w, b, u), LANES) for u in sides]
        unit_lanes = pl.ds(spot(w, b), WIDE)

        top = [jnp.full((8, LANES), MASKED, F32) for _ in sides]
        for first, n in TILES:
            at = slice(first, first + n)
            add = bias[pl.ds(aligned(b * MET + first, ROWS), n), :]
            add = jnp.concatenate([add] * CH, axis=1)
            kb = ks[tile(b, first, n), :]
            for u in sides:
                sc = jnp.dot(kb, qt[:, lanes[u]], preferred_element_type=F32)
                sc = sc * EXP2_SCALE + add
                s_buf[u, at, :] = sc
                top[u] = jnp.maximum(top[u], jnp.max(groups(sc), axis=0))
        top = [jnp.max(x, axis=0, keepdims=True) for x in top]
        sums = [jnp.zeros((8, LANES), F32) for _ in sides]
        dots = [jnp.zeros((8, LANES), F32) for _ in sides]
        for first, n in TILES:
            at = slice(first, first + n)
            vb = vs[tile(b, first, n), :]
            for u in sides:
                gp = jnp.dot(vb, gt[:, lanes[u]], preferred_element_type=F32)
                w2 = jnp.exp2(s_buf[u, at, :] - top[u])
                gp_buf[u, at, :] = gp
                sums[u] = sums[u] + jnp.sum(groups(w2), axis=0)
                dots[u] = dots[u] + jnp.sum(groups(w2 * gp), axis=0)
        sums = [jnp.sum(x, axis=0, keepdims=True) for x in sums]
        mean = [jnp.sum(x, axis=0, keepdims=True) / r for x, r in zip(dots, sums)]
        less = [m + jnp.log(x) * math.log2(math.e) for m, x in zip(top, sums)]
        qrow = qr[unit_lanes, :]
        grow = gr[unit_lanes, :]
        ot = [jnp.zeros((D, LANES), F32) for _ in sides]
        dqt = [jnp.zeros((D, LANES), F32) for _ in sides]
        for first, n in TILES:
            at = slice(first, first + n)
            rows = tile(b, first, n)
            probs, grads = [], []
            for u in sides:
                prob = jnp.exp2(s_buf[u, at, :] - less[u])
                ds = (prob * (gp_buf[u, at, :] - mean[u])).astype(BF16)
                prob = prob.astype(BF16)
                if not held:
                    ot[u] += jnp.dot(vt[:, rows], prob, preferred_element_type=F32)
                    dqt[u] += jnp.dot(kt[:, rows], ds, preferred_element_type=F32)
                probs.append(prob)
                grads.append(ds)
            prob = jnp.concatenate(probs, axis=1)
            ds = jnp.concatenate(grads, axis=1)
            if held:
                p_hold[at, :] = prob
                ds_hold[at, :] = ds
            if first >= CACHE:
                dk[rows, :] += jnp.dot(ds, qrow, preferred_element_type=F32)
                dv[rows, :] += jnp.dot(prob, grow, preferred_element_type=F32)
        if not held:
            for u in sides:
                close(w, u, b, ot[u], dqt[u])

    def rest(w, b):
        for u in sides:
            part = slice(u * LANES, (u + 1) * LANES)
            ot = jnp.zeros((D, LANES), F32)
            dqt = jnp.zeros((D, LANES), F32)
            for first, n in TILES:
                at = slice(first, first + n)
                rows = tile(b, first, n)
                ot += jnp.dot(vt[:, rows], p_hold[at, part], preferred_element_type=F32)
                dqt += jnp.dot(kt[:, rows], ds_hold[at, part], preferred_element_type=F32)
            close(w, u, b, ot, dqt)

    def close(w, u, b, ot, dqt):
        here = pl.ds(aligned(b * ROWS, ROWS), ROWS)
        now = pl.ds(aligned(2 * SLAB + b * ROWS, ROWS), ROWS)
        cos = cos_buf[:, now]
        sin = sin_buf[:, now]
        out = ot.astype(BF16)
        back = (dqt * SCALE).astype(BF16).astype(F32)
        for h in range(CH):
            cols = pl.ds(aligned(w * WIDE + u * LANES + h * D, D), D)
            part = slice(h * D, (h + 1) * D)
            oh[here, cols] = out[:, part].T
            x = xt[:, pl.ds(aligned(spot(w, b, u) + h * D, D), D)].astype(F32)
            dx, term = norm_backward(x, gain_buf[...], back[:, part], cos, sin)
            gacc[...] += term
            dqh[here, cols] = dx.astype(BF16).T

    def out_copies(w, d):
        yt = lax.rem(y + d, NY)
        return [
            remote(
                x.at[pl.ds(yt * ROWS, ROWS), pl.ds(w * WIDE, WIDE)],
                buf.at[:, pl.ds(y * COLS + w * WIDE, WIDE)],
                osend.at[a, w, d - 1],
                orecv.at[a, w, d - 1],
                z,
                yt,
            )
            for a, (x, buf) in enumerate(((oh, oa), (dqh, oq)))
        ]

    def out_stays(w):
        return [
            pltpu.make_async_copy(
                x.at[here, pl.ds(w * WIDE, WIDE)],
                buf.at[:, pl.ds(y * COLS + w * WIDE, WIDE)],
                olocal.at[a, w],
            )
            for a, (x, buf) in enumerate(((oh, oa), (dqh, oq)))
        ]

    d_last = jnp.where(y == 0, 3, jnp.where(y == 1, 1, 0))

    def await_unit(w, d):
        @pl.when(d > 0)
        def _():
            for copy in query_copies(w, NY - d):
                copy.wait_recv()

    def leave_unit(w, d):
        @pl.when(d > 0)
        def _():
            for copy in out_copies(w, d):
                copy.start()

        @pl.when(d == 0)
        def _():
            for copy in out_stays(w):
                copy.start()

    def step(n, carry):
        w = jnp.where((n == 3) | (n == 4) | (n == 6), 1, 0)
        d = jnp.where(n == 0, 0, jnp.where(n > 4, 2, jnp.where((n == 1) | (n == 3), 1, 3)))
        d = jnp.where(((n == 3) | (n == 4)) & (d == d_last), 0, d)
        b = lax.rem(y + d, NY)

        @pl.when(n > 0)
        def _():
            await_unit(w, d)
            prepare(w, b)

        attend(w, b)
        leave_unit(w, d)
        return carry

    lax.fori_loop(0, 7, step, 0)

    half = SLAB // 2
    lower, upper = slice(0, half), slice(half, SLAB)
    sums = ((dk, dkh, rk, SCALE), (dv, dvh, rv, 1.0))

    def back(i, hop, h):
        low, got = sums[i][1], sums[i][2]
        part = pl.ds(h * half, half)
        return remote(
            low.at[h] if hop == 0 else got.at[0, part, :],
            got.at[hop, part, :],
            hsend.at[i, hop, h],
            hrecv.at[i, hop, h],
            before,
            y,
        )

    def first_hop(h):
        for i, (total, low, _, scale) in enumerate(sums):
            rows = slice(CACHE + h * half, CACHE + (h + 1) * half)
            low[h] = (total[rows, :] * scale).astype(BF16)
            back(i, 0, h).start()

    def second_hop(h):
        for i, (total, _, got, scale) in enumerate(sums):
            back(i, 0, h).wait_recv()
            rows = slice(CACHE + SLAB + h * half, CACHE + SLAB + (h + 1) * half)
            at = (lower, upper)[h]
            mid = total[rows, :] * scale + got[0, at, :].astype(F32)
            got[0, at, :] = mid.astype(BF16)
            back(i, 1, h).start()

    first_hop(0)
    b_last = lax.rem(y + d_last, NY)
    await_unit(1, d_last)
    prepare(1, b_last)
    attend(1, b_last, True)
    first_hop(1)
    second_hop(0)
    rest(1, b_last)
    leave_unit(1, d_last)

    terms = jnp.zeros((D, ROWS), F32)
    for slab in range(3):
        rows = slice(slab * SLAB, (slab + 1) * SLAB)
        dkt = (dk[CACHE + slab * SLAB : CACHE + (slab + 1) * SLAB, :] * SCALE).T
        a, b = rotate(dkt[:HALF], dkt[HALF:], cos_buf[:, rows], -sin_buf[:, rows])
        term = jnp.concatenate([a, b], axis=0) * kx[:, rows]
        for i in range(SLAB // ROWS):
            terms = terms + term[:, i * ROWS : (i + 1) * ROWS]
    rows = [jnp.sum(x.T, axis=0, keepdims=True) for x in (gacc[...], terms)]
    total = jnp.concatenate(rows + [jnp.zeros((6, D), F32)], axis=0)

    def share(buf, me, n, first, total, device):
        buf[me] = total
        copies = []
        for d in range(1, n):
            copies.append(
                pltpu.make_async_remote_copy(
                    src_ref=buf.at[me],
                    dst_ref=buf.at[me],
                    send_sem=gsend.at[first + d - 1],
                    recv_sem=grecv.at[first + d - 1],
                    device_id=device(lax.rem(me + d, n)),
                    device_id_type=pl.DeviceIdType.MESH,
                )
            )
            copies[-1].start()
        return copies

    def add_up(copies, buf, n):
        for copy in copies:
            copy.wait()
        total = buf[0]
        for i in range(1, n):
            total = total + buf[i]
        return total

    second_hop(1)
    shared = share(gx, dp, ndp, NY + NZ - 2, total, lambda to: {"dp": to})
    kv_out = []

    def leave_row(i, x, buf):
        there = buf.at[:, pl.ds(y * D, D)]
        copies = []
        for d in hops:
            yt = lax.rem(y + d, NY)
            copies.append(
                remote(
                    x.at[pl.ds(yt * ROWS, ROWS), :],
                    there,
                    bsend.at[i, d - 1],
                    brecv.at[i, d - 1],
                    z,
                    yt,
                )
            )
        copies.append(pltpu.make_async_copy(x.at[here, :], there, local.at[i]))
        for copy in copies:
            copy.start()
        kv_out.extend(copies)

    total = add_up(shared, gx, ndp)
    shared = share(gz, z, NZ, NY - 1, total, lambda to: {"context": to * NY + y})
    for h in range(2):
        back(0, 1, h).wait_recv()
        at = (lower, upper)[h]
        rows = slice(own + h * half, own + (h + 1) * half)
        raw = slice(2 * SLAB + h * half, 2 * SLAB + (h + 1) * half)
        dkt = (dk[rows, :] * SCALE + rk[1, at, :].astype(F32)).T
        dx, _ = norm_backward(
            kraw[raw, :].T.astype(F32), kgain_col, dkt, cos_buf[:, raw], sin_buf[:, raw]
        )
        kg[at, :] = dx.astype(BF16).T
    leave_row(0, kg, okg)
    total = add_up(shared, gz, NZ)
    shared = share(gy, y, NY, 0, total, lambda to: {"context": z * NY + to})
    for h in range(2):
        back(1, 1, h).wait_recv()
    vg[...] = (dv[own:, :] + rv[1].astype(F32)).astype(BF16)
    leave_row(1, vg, ovg)
    gains_out[...] = add_up(shared, gy, NY)[:2]

    for w in range(2):
        for d in hops:
            for copy in out_copies(w, d):
                copy.wait()
            for copy in query_copies(w, d):
                copy.wait_send()
        for copy in out_stays(w):
            copy.wait()
    leaving = [
        pltpu.make_async_copy(oa, attn_out, local.at[2]),
        pltpu.make_async_copy(oq, dq_out, local.at[3]),
    ]
    for copy in leaving:
        copy.start()
    for copy in kv_out:
        copy.wait()
    for i, (x, out) in enumerate(((okg, kg_out), (ovg, vg_out))):
        copy = pltpu.make_async_copy(x, out, local.at[4 + i])
        copy.start()
        leaving.append(copy)
    for copies in (ycopies, zcopies):
        for copy in copies.values():
            copy.wait_send()
    for i in range(2):
        for hop in range(2):
            for h in range(2):
                back(i, hop, h).wait_send()
    for copy in leaving:
        copy.wait()


def finish_kernel(*refs):
    n = (len(refs) - 1) // 3
    sems = refs[-1]
    into, out = [], []
    for i in range(n):
        rows = refs[i].shape[0]
        size = rows // 4 if i < 2 else rows
        for first in range(0, rows, size):
            at = pl.ds(first, size)
            held = refs[2 * n + i].at[at, :]
            sem = len(into)
            into.append(pltpu.make_async_copy(refs[i].at[at, :], held, sems.at[0, sem]))
            out.append(pltpu.make_async_copy(held, refs[n + i].at[at, :], sems.at[1, sem]))
    for copy in into:
        copy.start()
    for a, b in zip(into, out):
        a.wait()
        b.start()
    for copy in out:
        copy.wait()


VMEM = pl.BlockSpec(memory_space=pltpu.VMEM)
HBM = pl.BlockSpec(memory_space=pltpu.HBM)
ANY = pl.BlockSpec(memory_space=pl.ANY)
DMA = pltpu.SemaphoreType.DMA


def body(queries, keys, values, pkeys, pvalues, out_grad, query_gain, key_gain, lengths, offsets):
    ndp = lax.axis_size("dp")
    sd = jax.ShapeDtypeStruct

    def vmem(shape, dtype, count=1):
        return [pltpu.VMEM(shape, dtype)] * count

    def dma(shape, count=2):
        return [DMA(shape)] * count

    results = pl.pallas_call(
        functools.partial(fused_kernel, ndp),
        name="fused",
        out_shape=(
            sd((ROWS, NY * COLS), BF16),
            sd((ROWS, NY * COLS), BF16),
            sd((ROWS, NY * D), BF16),
            sd((ROWS, NY * D), BF16),
            sd((2, D), F32),
        ),
        in_specs=[HBM] * 2 + [VMEM] * 2 + [HBM] * 6,
        out_specs=(ANY, ANY, ANY, ANY, VMEM),
        scratch_shapes=vmem((SLAB, COLS), BF16, 2)
        + vmem((KEYS, D), BF16, 2)
        + vmem((D, KEYS), BF16, 2)
        + vmem((WINDOW, D), BF16)
        + vmem((D, WINDOW), F32)
        + vmem((HALF, WINDOW), F32, 2)
        + vmem((D, D), F32)
        + vmem((NY * MET, ROWS), F32)
        + vmem((D, HQ * SLAB), BF16, 3)
        + vmem((HQ * SLAB, D), BF16, 2)
        + vmem((2, MET, LANES), F32, 2)
        + vmem((MET, WIDE), BF16, 2)
        + vmem((KEYS, D), F32, 2)
        + vmem((D, ROWS), F32)
        + vmem((SLAB, COLS), BF16, 2)
        + vmem((ROWS, NY * COLS), BF16, 2)
        + vmem((ROWS, NY * D), BF16, 2)
        + vmem((2, SLAB, D), BF16, 2)
        + vmem((2, SLAB // 2, D), BF16, 2)
        + vmem((SLAB, D), BF16, 2)
        + vmem((NY, 8, D), F32)
        + vmem((NZ, 8, D), F32)
        + vmem((ndp, 8, D), F32)
        + [pltpu.SMEM((1, SEGS), jnp.int32)] * 2
        + dma((2,), 1)
        + dma((4, NY - 1))
        + dma((2, 2, NY - 1))
        + dma((2,))
        + dma((2, NY))
        + dma((2, NZ - 1))
        + dma((2, 2, NY - 1))
        + dma((2, NY - 1))
        + dma((2, 2, 2))
        + dma((NY + NZ + ndp - 3,))
        + dma((6,), 1)
        + dma((2, 2), 1),
        compiler_params=pltpu.CompilerParams(
            collective_id=0, has_side_effects=True, vmem_limit_bytes=62 << 20
        ),
    )(
        lengths,
        offsets,
        query_gain.reshape(1, D),
        key_gain.reshape(1, D),
        queries[0],
        out_grad[0],
        keys[0],
        values[0],
        pkeys[0],
        pvalues[0],
    )
    attention, query_grad, key_grad, value_grad, gains = pl.pallas_call(
        finish_kernel,
        name="finish",
        out_shape=[sd(x.shape, x.dtype) for x in results],
        in_specs=[ANY] * 5,
        out_specs=[HBM] * 5,
        scratch_shapes=[pltpu.VMEM(x.shape, x.dtype) for x in results] + [DMA((2, 11))],
        compiler_params=pltpu.CompilerParams(vmem_limit_bytes=62 << 20),
    )(*results)
    return attention[None], query_grad[None], key_grad[None], value_grad[None], gains


def solution(mesh):
    rows = P("dp", "context", None)
    in_specs = (rows,) * 6 + (P(), P(), P("dp", None), P("dp", None))
    out_specs = (rows,) * 4 + (P(),)
    return jax.shard_map(body, mesh=mesh, in_specs=in_specs, out_specs=out_specs, check_vma=False)
```

```python
import functools
import math

import jax
import jax.numpy as jnp
from jax import lax
from jax.experimental import pallas as pl
from jax.experimental.pallas import tpu as pltpu
from jax.sharding import PartitionSpec as P

EPSILON = 1e-06
ROPE_BASE = 1000000.0
D = 128
HALF = D // 2
HQ = 8
NY = 4
NZ = 8
ROWS = 128
SLAB = NY * ROWS
COLS = HQ * D
CACHE = 512
CPART = CACHE // (NY * NZ)
WINDOW = 3 * SLAB
KEYS = CACHE + WINDOW
SEGS = 8
REACH = SLAB * 2 + ROWS
MET = CACHE + REACH
CH = 2
NC = HQ // CH
LANES = CH * D
WIDE = 2 * LANES
TILES = ((0, 512), (512, 512), (1024, 512), (1536, 128))
SCALE = 1.0 / math.sqrt(D)
EXP2_SCALE = SCALE * math.log2(math.e)
MASKED = -1e30
F32 = jnp.float32
BF16 = jnp.bfloat16


def aligned(x, n):
    return x if isinstance(x, int) else pl.multiple_of(x, n)


def place():
    c = lax.axis_index("context")
    return lax.div(c, NY), lax.rem(c, NY)


def remote(src, dst, send, recv, z, y):
    return pltpu.make_async_remote_copy(
        src_ref=src,
        dst_ref=dst,
        send_sem=send,
        recv_sem=recv,
        device_id={"context": z * NY + y},
        device_id_type=pl.DeviceIdType.MESH,
    )


def greet_plane(z, y):
    barrier = pltpu.get_barrier_semaphore()
    for d in range(1, NY):
        pl.semaphore_signal(
            barrier,
            inc=1,
            device_id={"context": z * NY + lax.rem(y + d, NY)},
            device_id_type=pl.DeviceIdType.MESH,
        )
    for d in range(1, NZ):
        pl.semaphore_signal(
            barrier,
            inc=1,
            device_id={"context": lax.rem(z + d, NZ) * NY + y},
            device_id_type=pl.DeviceIdType.MESH,
        )
    return barrier


def rotate(a, b, cos, sin):
    return a * cos - b * sin, b * cos + a * sin


def column(row_ref):
    return jnp.broadcast_to(row_ref[...], (D, D)).T


def norm_forward(xt, gain):
    r = lax.rsqrt(jnp.mean(xt * xt, axis=0, keepdims=True) + EPSILON)
    return xt * r * gain


def norm_backward(xt, gain, dyt, cos, sin):
    r = lax.rsqrt(jnp.mean(xt * xt, axis=0, keepdims=True) + EPSILON)
    xh = xt * r
    d1, d2 = dyt[:HALF], dyt[HALF:]
    dn = jnp.concatenate([d1 * cos + d2 * sin, d2 * cos - d1 * sin], axis=0)
    dxh = dn * gain
    dx = r * (dxh - xh * jnp.mean(dxh * xh, axis=0, keepdims=True))
    return dx, dn * xh


def fetch_pieces(lengths_in, offsets_in, lengths, offsets, sems):
    copies = [
        pltpu.make_async_copy(lengths_in, lengths, sems.at[0]),
        pltpu.make_async_copy(offsets_in, offsets, sems.at[1]),
    ]
    for copy in copies:
        copy.start()
    return copies


def fused_kernel(
    ndp,
    lengths_in,
    offsets_in,
    qgain,
    kgain,
    q,
    g,
    k,
    v,
    pk,
    pv,
    attn_out,
    dq_out,
    kg_out,
    vg_out,
    gains_out,
    qs,
    gs,
    ks,
    vs,
    kt,
    vt,
    kraw,
    kx,
    cos_buf,
    sin_buf,
    gain_buf,
    bias,
    xt,
    qt,
    gt,
    qr,
    gr,
    s_buf,
    gp_buf,
    p_hold,
    ds_hold,
    dk,
    dv,
    gacc,
    oh,
    dqh,
    oa,
    oq,
    okg,
    ovg,
    rk,
    rv,
    dkh,
    dvh,
    kg,
    vg,
    gy,
    gz,
    gx,
    lengths,
    offsets,
    psems,
    ysend,
    yrecv,
    qsend,
    qrecv,
    zsend,
    zrecv,
    nsend,
    nrecv,
    csend,
    crecv,
    osend,
    orecv,
    bsend,
    brecv,
    hsend,
    hrecv,
    gsend,
    grecv,
    local,
    olocal,
):
    z, y = place()
    dp = lax.axis_index("dp")
    pieces = fetch_pieces(lengths_in, offsets_in, lengths, offsets, psems)
    barrier = greet_plane(z, y)
    for d in range(1, ndp):
        pl.semaphore_signal(
            barrier,
            inc=1,
            device_id={"dp": lax.rem(dp + d, ndp)},
            device_id_type=pl.DeviceIdType.MESH,
        )
    after, before = lax.rem(z + 1, NZ), lax.rem(z + NZ - 1, NZ)
    for d in range(1, NY):
        pl.semaphore_signal(
            barrier,
            inc=1,
            device_id={"context": before * NY + lax.rem(y + d, NY)},
            device_id_type=pl.DeviceIdType.MESH,
        )
    pl.semaphore_wait(barrier, NY - 1 + NZ - 1 + ndp - 1 + NY - 1)

    own = CACHE + 2 * SLAB
    crow = z * (NY * CPART)
    hops = (2, 1, 3)

    def parts(head, row):
        one = pl.ds(head * D, D)
        cached = pl.ds(crow + row * CPART, CPART)
        return [
            (k.at[:, one], kraw.at[pl.ds(2 * SLAB + row * ROWS, ROWS), :]),
            (v.at[:, one], vs.at[pl.ds(own + row * ROWS, ROWS), :]),
            (pk.at[:, one], ks.at[cached, :]),
            (pv.at[:, one], vs.at[cached, :]),
        ]

    mine = [
        pltpu.make_async_copy(src, dst, local.at[i])
        for i, (src, dst) in enumerate(parts(y, y))
    ]
    ycopies = {}
    zcopies = {}

    def send(i):
        for d in hops:
            yt = lax.rem(y + d, NY)
            src, dst = parts(yt, y)[i]
            copy = remote(src, dst, ysend.at[i, d - 1], yrecv.at[i, d - 1], z, yt)
            copy.start()
            ycopies[i, d] = copy
        mine[i].start()

    def arrived(i):
        mine[i].wait()
        for d in hops:
            ycopies[i, d].wait_recv()

    def send_after(j):
        buf, top = ((kraw, SLAB), (vs, own - SLAB))[j]
        for d in range(NY):
            yt = lax.rem(y + d, NY)
            copy = remote(
                parts(yt, y)[j][0],
                buf.at[pl.ds(top + y * ROWS, ROWS), :],
                nsend.at[j, d],
                nrecv.at[j, d],
                after,
                yt,
            )
            copy.start()
            zcopies[j, d, "next"] = copy

    for j in range(2):
        send_after(j)
    for i in (2, 3, 0, 1):
        send(i)

    whole = pl.ds(y * COLS, COLS)
    here = pl.ds(y * ROWS, ROWS)
    mine_q = [
        pltpu.make_async_copy(x.at[:, whole], buf.at[here, :], local.at[4 + a])
        for a, (x, buf) in enumerate(((q, qs), (g, gs)))
    ]

    def query_copies(w, d):
        yt = lax.rem(y + d, NY)
        return [
            remote(
                x.at[:, pl.ds(yt * COLS + w * WIDE, WIDE)],
                buf.at[here, pl.ds(w * WIDE, WIDE)],
                qsend.at[a, w, d - 1],
                qrecv.at[a, w, d - 1],
                z,
                yt,
            )
            for a, (x, buf) in enumerate(((q, qs), (g, gs)))
        ]

    def send_queries(ways):
        for w, d in ways:
            for copy in query_copies(w, d):
                copy.start()

    for copy in mine_q:
        copy.start()
    send_queries(((0, 3), (0, 1), (1, 3), (1, 1)))

    for copy in pieces:
        copy.wait()

    def per_token(t):
        first = run = jnp.int32(0)
        low = jnp.zeros_like(t)
        clo = jnp.zeros_like(t)
        chi = jnp.zeros_like(t)
        for s in range(SEGS):
            end = first + lengths[0, s]
            stop = run + offsets[0, s]
            inside = (t >= first) & (t < end)
            low = jnp.where(inside, first, low)
            clo = jnp.where(inside, run, clo)
            chi = jnp.where(inside, stop, chi)
            first, run = end, stop
        return low, clo, chi

    t = (z - 2) * SLAB + lax.broadcasted_iota(jnp.int32, (1, WINDOW), 1)
    low, clo, chi = per_token(t)
    frequency = jnp.exp(
        lax.broadcasted_iota(jnp.int32, (HALF, 1), 0).astype(F32)
        * (-2.0 * math.log(ROPE_BASE) / D)
    )
    angles = frequency * (t - low + chi - clo).astype(F32)

    def forward(j):
        x, top = ((kraw, SLAB), (vs, own - SLAB))[j]
        copy = remote(
            x.at[pl.ds(top, SLAB), :],
            x.at[pl.ds(top - SLAB, SLAB), :],
            zsend.at[j],
            zrecv.at[j],
            after,
            y,
        )
        copy.start()
        zcopies[j, "far"] = copy

    kgain_col = column(kgain)[:, :1]

    def rotate_keys(slab):
        rows = slice(slab * SLAB, (slab + 1) * SLAB)
        met = slice(CACHE + slab * SLAB, CACHE + (slab + 1) * SLAB)
        x = kraw[rows, :].T.astype(F32)
        xh = x * lax.rsqrt(jnp.mean(x * x, axis=0, keepdims=True) + EPSILON)
        kx[:, rows] = xh
        n = xh * kgain_col
        a, b = rotate(n[:HALF], n[HALF:], cos_buf[:, rows], sin_buf[:, rows])
        rotated = jnp.concatenate([a, b], axis=0).astype(BF16)
        kt[:, met] = rotated
        ks[met, :] = rotated.T

    cos_buf[...] = jnp.cos(angles)
    sin_buf[...] = jnp.sin(angles)
    gain_buf[...] = column(qgain)
    def cached_to(j, i, rows, d):
        part = (ks, vs)[j].at[rows, :]
        zt = lax.rem(z + d, NZ)
        copy = remote(part, part, csend.at[j, i], crecv.at[j, i], zt, y)
        copy.start()
        zcopies[j, i, "cached"] = copy

    def pass_next(j):
        for d in range(NY):
            zcopies[j, d, "next"].wait_recv()
        forward(j)

    pass_next(0)
    for j in range(2):
        arrived(2 + j)
        for i, d in enumerate((1, 2, 5, 6, 7)):
            cached_to(j, i, pl.ds(crow, NY * CPART), d)
    pass_next(1)
    send_queries(((0, 2), (1, 2)))

    def mask(b, carry):
        t = z * SLAB + b * ROWS + lax.broadcasted_iota(jnp.int32, (1, ROWS), 1)
        low, clo, chi = per_token(t)
        rows = lax.broadcasted_iota(jnp.int32, (CACHE, ROWS), 0)
        base = aligned(b * MET, ROWS)
        seen = (rows >= clo) & (rows < chi)
        bias[pl.ds(base, CACHE), :] = jnp.where(seen, 0.0, MASKED)
        rows = lax.broadcasted_iota(jnp.int32, (REACH, ROWS), 0)
        token = rows + ((z - 2) * SLAB + b * ROWS)
        seen = (token >= low) & (token <= t)
        base = aligned(b * MET + CACHE, ROWS)
        bias[pl.ds(base, REACH), :] = jnp.where(seen, 0.0, MASKED)
        return carry

    lax.fori_loop(0, NY, mask, 0)
    dk[...] = jnp.zeros_like(dk)
    dv[...] = jnp.zeros_like(dv)
    gacc[...] = jnp.zeros_like(gacc)

    arrived(0)
    rotate_keys(2)
    arrived(1)
    vt[:, own:] = vs[own:, :].T
    for j in range(2):
        zcopies[j, 2, "cached"].wait_recv()
        for i, d in ((5, 7), (6, 6)):
            cached_to(j, i, pl.ds(lax.rem(z + 3, NZ) * (NY * CPART), NY * CPART), d)
    rotate_keys(1)
    vt[:, CACHE + SLAB : own] = vs[CACHE + SLAB : own, :].T

    def spot(w, b, u=0):
        return aligned((w * NY + b) * WIDE + u * LANES, LANES)

    def prepare(w, b):
        rows = pl.ds(aligned(b * ROWS, ROWS), ROWS)
        now = pl.ds(aligned(2 * SLAB + b * ROWS, ROWS), ROWS)
        cos = cos_buf[:, now]
        sin = sin_buf[:, now]
        for h in range(2 * CH):
            cols = pl.ds(aligned(w * WIDE + h * D, D), D)
            lanes = pl.ds(aligned(spot(w, b) + h * D, D), D)
            x = qs[rows, cols].T
            xt[:, lanes] = x
            n = norm_forward(x.astype(F32), gain_buf[...])
            r1, r2 = rotate(n[:HALF], n[HALF:], cos, sin)
            rot = jnp.concatenate([r1, r2], axis=0).astype(BF16)
            qt[:, lanes] = rot
            qr[lanes, :] = rot.T
            grad = gs[rows, cols]
            gr[lanes, :] = grad
            gt[:, lanes] = grad.T

    for copy in mine_q:
        copy.wait()

    for j, (x, xtr) in enumerate(((ks, kt), (vs, vt))):
        for i in range(NZ - 1):
            if i != 2:
                zcopies[j, i, "cached"].wait_recv()
        xtr[:, :CACHE] = x[:CACHE, :].T
    prepare(0, y)
    zcopies[0, "far"].wait_recv()
    rotate_keys(0)
    zcopies[1, "far"].wait_recv()
    vt[:, CACHE : CACHE + SLAB] = vs[CACHE : CACHE + SLAB, :].T

    def groups(x):
        return x.reshape(x.shape[0] // 8, 8, LANES)

    sides = range(2)

    def tile(b, first, rows):
        if first < CACHE:
            return pl.ds(first, rows)
        return pl.ds(aligned(first + b * ROWS, ROWS), rows)

    def attend(w, b, held=False):
        lanes = [pl.ds(spot(w, b, u), LANES) for u in sides]
        unit_lanes = pl.ds(spot(w, b), WIDE)

        top = [jnp.full((8, LANES), MASKED, F32) for _ in sides]
        for first, n in TILES:
            at = slice(first, first + n)
            add = bias[pl.ds(aligned(b * MET + first, ROWS), n), :]
            add = jnp.concatenate([add] * CH, axis=1)
            kb = ks[tile(b, first, n), :]
            for u in sides:
                sc = jnp.dot(kb, qt[:, lanes[u]], preferred_element_type=F32)
                sc = sc * EXP2_SCALE + add
                s_buf[u, at, :] = sc
                top[u] = jnp.maximum(top[u], jnp.max(groups(sc), axis=0))
        top = [jnp.max(x, axis=0, keepdims=True) for x in top]
        sums = [jnp.zeros((8, LANES), F32) for _ in sides]
        dots = [jnp.zeros((8, LANES), F32) for _ in sides]
        for first, n in TILES:
            at = slice(first, first + n)
            vb = vs[tile(b, first, n), :]
            for u in sides:
                gp = jnp.dot(vb, gt[:, lanes[u]], preferred_element_type=F32)
                w2 = jnp.exp2(s_buf[u, at, :] - top[u])
                gp_buf[u, at, :] = gp
                sums[u] = sums[u] + jnp.sum(groups(w2), axis=0)
                dots[u] = dots[u] + jnp.sum(groups(w2 * gp), axis=0)
        sums = [jnp.sum(x, axis=0, keepdims=True) for x in sums]
        mean = [jnp.sum(x, axis=0, keepdims=True) / r for x, r in zip(dots, sums)]
        less = [m + jnp.log(x) * math.log2(math.e) for m, x in zip(top, sums)]
        qrow = qr[unit_lanes, :]
        grow = gr[unit_lanes, :]
        ot = [jnp.zeros((D, LANES), F32) for _ in sides]
        dqt = [jnp.zeros((D, LANES), F32) for _ in sides]
        for first, n in TILES:
            at = slice(first, first + n)
            rows = tile(b, first, n)
            probs, grads = [], []
            for u in sides:
                prob = jnp.exp2(s_buf[u, at, :] - less[u])
                ds = (prob * (gp_buf[u, at, :] - mean[u])).astype(BF16)
                prob = prob.astype(BF16)
                if not held:
                    ot[u] += jnp.dot(vt[:, rows], prob, preferred_element_type=F32)
                    dqt[u] += jnp.dot(kt[:, rows], ds, preferred_element_type=F32)
                probs.append(prob)
                grads.append(ds)
            prob = jnp.concatenate(probs, axis=1)
            ds = jnp.concatenate(grads, axis=1)
            if held:
                p_hold[at, :] = prob
                ds_hold[at, :] = ds
            if first >= CACHE:
                dk[rows, :] += jnp.dot(ds, qrow, preferred_element_type=F32)
                dv[rows, :] += jnp.dot(prob, grow, preferred_element_type=F32)
        if not held:
            for u in sides:
                close(w, u, b, ot[u], dqt[u])

    def rest(w, b):
        for u in sides:
            part = slice(u * LANES, (u + 1) * LANES)
            ot = jnp.zeros((D, LANES), F32)
            dqt = jnp.zeros((D, LANES), F32)
            for first, n in TILES:
                at = slice(first, first + n)
                rows = tile(b, first, n)
                ot += jnp.dot(vt[:, rows], p_hold[at, part], preferred_element_type=F32)
                dqt += jnp.dot(kt[:, rows], ds_hold[at, part], preferred_element_type=F32)
            close(w, u, b, ot, dqt)

    def close(w, u, b, ot, dqt):
        here = pl.ds(aligned(b * ROWS, ROWS), ROWS)
        now = pl.ds(aligned(2 * SLAB + b * ROWS, ROWS), ROWS)
        cos = cos_buf[:, now]
        sin = sin_buf[:, now]
        out = ot.astype(BF16)
        back = (dqt * SCALE).astype(BF16).astype(F32)
        for h in range(CH):
            cols = pl.ds(aligned(w * WIDE + u * LANES + h * D, D), D)
            part = slice(h * D, (h + 1) * D)
            oh[here, cols] = out[:, part].T
            x = xt[:, pl.ds(aligned(spot(w, b, u) + h * D, D), D)].astype(F32)
            dx, term = norm_backward(x, gain_buf[...], back[:, part], cos, sin)
            gacc[...] += term
            dqh[here, cols] = dx.astype(BF16).T

    def out_copies(w, d):
        yt = lax.rem(y + d, NY)
        return [
            remote(
                x.at[pl.ds(yt * ROWS, ROWS), pl.ds(w * WIDE, WIDE)],
                buf.at[:, pl.ds(y * COLS + w * WIDE, WIDE)],
                osend.at[a, w, d - 1],
                orecv.at[a, w, d - 1],
                z,
                yt,
            )
            for a, (x, buf) in enumerate(((oh, oa), (dqh, oq)))
        ]

    def out_stays(w):
        return [
            pltpu.make_async_copy(
                x.at[here, pl.ds(w * WIDE, WIDE)],
                buf.at[:, pl.ds(y * COLS + w * WIDE, WIDE)],
                olocal.at[a, w],
            )
            for a, (x, buf) in enumerate(((oh, oa), (dqh, oq)))
        ]

    d_last = jnp.where(y == 0, 3, jnp.where(y == 1, 1, 0))

    def await_unit(w, d):
        @pl.when(d > 0)
        def _():
            for copy in query_copies(w, NY - d):
                copy.wait_recv()

    def leave_unit(w, d):
        @pl.when(d > 0)
        def _():
            for copy in out_copies(w, d):
                copy.start()

        @pl.when(d == 0)
        def _():
            for copy in out_stays(w):
                copy.start()

    def step(n, carry):
        w = jnp.where((n == 3) | (n == 4) | (n == 6), 1, 0)
        d = jnp.where(n == 0, 0, jnp.where(n > 4, 2, jnp.where((n == 1) | (n == 3), 1, 3)))
        d = jnp.where(((n == 3) | (n == 4)) & (d == d_last), 0, d)
        b = lax.rem(y + d, NY)

        @pl.when(n > 0)
        def _():
            await_unit(w, d)
            prepare(w, b)

        attend(w, b)
        leave_unit(w, d)
        return carry

    lax.fori_loop(0, 7, step, 0)

    half = SLAB // 2
    lower, upper = slice(0, half), slice(half, SLAB)
    sums = ((dk, dkh, rk, SCALE), (dv, dvh, rv, 1.0))

    def back(i, hop, h):
        low, got = sums[i][1], sums[i][2]
        part = pl.ds(h * half, half)
        return remote(
            low.at[h] if hop == 0 else got.at[0, part, :],
            got.at[hop, part, :],
            hsend.at[i, hop, h],
            hrecv.at[i, hop, h],
            before,
            y,
        )

    def first_hop(h):
        for i, (total, low, _, scale) in enumerate(sums):
            rows = slice(CACHE + h * half, CACHE + (h + 1) * half)
            low[h] = (total[rows, :] * scale).astype(BF16)
            back(i, 0, h).start()

    def second_hop(h):
        for i, (total, _, got, scale) in enumerate(sums):
            back(i, 0, h).wait_recv()
            rows = slice(CACHE + SLAB + h * half, CACHE + SLAB + (h + 1) * half)
            at = (lower, upper)[h]
            mid = total[rows, :] * scale + got[0, at, :].astype(F32)
            got[0, at, :] = mid.astype(BF16)
            back(i, 1, h).start()

    first_hop(0)
    b_last = lax.rem(y + d_last, NY)
    await_unit(1, d_last)
    prepare(1, b_last)
    attend(1, b_last, True)
    first_hop(1)
    second_hop(0)
    rest(1, b_last)
    leave_unit(1, d_last)

    terms = jnp.zeros((D, ROWS), F32)
    for slab in range(3):
        rows = slice(slab * SLAB, (slab + 1) * SLAB)
        dkt = (dk[CACHE + slab * SLAB : CACHE + (slab + 1) * SLAB, :] * SCALE).T
        a, b = rotate(dkt[:HALF], dkt[HALF:], cos_buf[:, rows], -sin_buf[:, rows])
        term = jnp.concatenate([a, b], axis=0) * kx[:, rows]
        for i in range(SLAB // ROWS):
            terms = terms + term[:, i * ROWS : (i + 1) * ROWS]
    rows = [jnp.sum(x.T, axis=0, keepdims=True) for x in (gacc[...], terms)]
    total = jnp.concatenate(rows + [jnp.zeros((6, D), F32)], axis=0)

    def share(buf, me, n, first, total, device):
        buf[me] = total
        copies = []
        for d in range(1, n):
            copies.append(
                pltpu.make_async_remote_copy(
                    src_ref=buf.at[me],
                    dst_ref=buf.at[me],
                    send_sem=gsend.at[first + d - 1],
                    recv_sem=grecv.at[first + d - 1],
                    device_id=device(lax.rem(me + d, n)),
                    device_id_type=pl.DeviceIdType.MESH,
                )
            )
            copies[-1].start()
        return copies

    def add_up(copies, buf, n):
        for copy in copies:
            copy.wait()
        total = buf[0]
        for i in range(1, n):
            total = total + buf[i]
        return total

    shared = share(gx, dp, ndp, NY + NZ - 2, total, lambda to: {"dp": to})
    second_hop(1)
    kv_out = []

    def leave_row(i, x, buf):
        there = buf.at[:, pl.ds(y * D, D)]
        copies = []
        for d in hops:
            yt = lax.rem(y + d, NY)
            copies.append(
                remote(
                    x.at[pl.ds(yt * ROWS, ROWS), :],
                    there,
                    bsend.at[i, d - 1],
                    brecv.at[i, d - 1],
                    z,
                    yt,
                )
            )
        copies.append(pltpu.make_async_copy(x.at[here, :], there, local.at[i]))
        for copy in copies:
            copy.start()
        kv_out.extend(copies)

    total = add_up(shared, gx, ndp)
    shared = share(gz, z, NZ, NY - 1, total, lambda to: {"context": to * NY + y})
    for h in range(2):
        back(0, 1, h).wait_recv()
        at = (lower, upper)[h]
        rows = slice(own + h * half, own + (h + 1) * half)
        raw = slice(2 * SLAB + h * half, 2 * SLAB + (h + 1) * half)
        dkt = (dk[rows, :] * SCALE + rk[1, at, :].astype(F32)).T
        dx, _ = norm_backward(
            kraw[raw, :].T.astype(F32), kgain_col, dkt, cos_buf[:, raw], sin_buf[:, raw]
        )
        kg[at, :] = dx.astype(BF16).T
    leave_row(0, kg, okg)
    total = add_up(shared, gz, NZ)
    shared = share(gy, y, NY, 0, total, lambda to: {"context": z * NY + to})
    for h in range(2):
        back(1, 1, h).wait_recv()
    vg[...] = (dv[own:, :] + rv[1].astype(F32)).astype(BF16)
    leave_row(1, vg, ovg)

    for w in range(2):
        for d in hops:
            for copy in out_copies(w, d):
                copy.wait()
            for copy in query_copies(w, d):
                copy.wait_send()
        for copy in out_stays(w):
            copy.wait()
    leaving = [
        pltpu.make_async_copy(oa, attn_out, local.at[2]),
        pltpu.make_async_copy(oq, dq_out, local.at[3]),
    ]
    for copy in leaving:
        copy.start()
    gains_out[...] = add_up(shared, gy, NY)[:2]
    for copy in kv_out:
        copy.wait()
    for i, (x, out) in enumerate(((okg, kg_out), (ovg, vg_out))):
        copy = pltpu.make_async_copy(x, out, local.at[4 + i])
        copy.start()
        leaving.append(copy)
    for copies in (ycopies, zcopies):
        for copy in copies.values():
            copy.wait_send()
    for i in range(2):
        for hop in range(2):
            for h in range(2):
                back(i, hop, h).wait_send()
    for copy in leaving:
        copy.wait()


def finish_kernel(*refs):
    n = (len(refs) - 1) // 3
    sems = refs[-1]
    into, out = [], []
    for i in range(n):
        rows = refs[i].shape[0]
        size = rows // 4 if i < 2 else rows
        for first in range(0, rows, size):
            at = pl.ds(first, size)
            held = refs[2 * n + i].at[at, :]
            sem = len(into)
            into.append(pltpu.make_async_copy(refs[i].at[at, :], held, sems.at[0, sem]))
            out.append(pltpu.make_async_copy(held, refs[n + i].at[at, :], sems.at[1, sem]))
    for copy in into:
        copy.start()
    for a, b in zip(into, out):
        a.wait()
        b.start()
    for copy in out:
        copy.wait()


VMEM = pl.BlockSpec(memory_space=pltpu.VMEM)
HBM = pl.BlockSpec(memory_space=pltpu.HBM)
ANY = pl.BlockSpec(memory_space=pl.ANY)
DMA = pltpu.SemaphoreType.DMA


def body(queries, keys, values, pkeys, pvalues, out_grad, query_gain, key_gain, lengths, offsets):
    ndp = lax.axis_size("dp")
    sd = jax.ShapeDtypeStruct

    def vmem(shape, dtype, count=1):
        return [pltpu.VMEM(shape, dtype)] * count

    def dma(shape, count=2):
        return [DMA(shape)] * count

    results = pl.pallas_call(
        functools.partial(fused_kernel, ndp),
        name="fused",
        out_shape=(
            sd((ROWS, NY * COLS), BF16),
            sd((ROWS, NY * COLS), BF16),
            sd((ROWS, NY * D), BF16),
            sd((ROWS, NY * D), BF16),
            sd((2, D), F32),
        ),
        in_specs=[HBM] * 2 + [VMEM] * 2 + [HBM] * 6,
        out_specs=(ANY, ANY, ANY, ANY, VMEM),
        scratch_shapes=vmem((SLAB, COLS), BF16, 2)
        + vmem((KEYS, D), BF16, 2)
        + vmem((D, KEYS), BF16, 2)
        + vmem((WINDOW, D), BF16)
        + vmem((D, WINDOW), F32)
        + vmem((HALF, WINDOW), F32, 2)
        + vmem((D, D), F32)
        + vmem((NY * MET, ROWS), F32)
        + vmem((D, HQ * SLAB), BF16, 3)
        + vmem((HQ * SLAB, D), BF16, 2)
        + vmem((2, MET, LANES), F32, 2)
        + vmem((MET, WIDE), BF16, 2)
        + vmem((KEYS, D), F32, 2)
        + vmem((D, ROWS), F32)
        + vmem((SLAB, COLS), BF16, 2)
        + vmem((ROWS, NY * COLS), BF16, 2)
        + vmem((ROWS, NY * D), BF16, 2)
        + vmem((2, SLAB, D), BF16, 2)
        + vmem((2, SLAB // 2, D), BF16, 2)
        + vmem((SLAB, D), BF16, 2)
        + vmem((NY, 8, D), F32)
        + vmem((NZ, 8, D), F32)
        + vmem((ndp, 8, D), F32)
        + [pltpu.SMEM((1, SEGS), jnp.int32)] * 2
        + dma((2,), 1)
        + dma((4, NY - 1))
        + dma((2, 2, NY - 1))
        + dma((2,))
        + dma((2, NY))
        + dma((2, NZ - 1))
        + dma((2, 2, NY - 1))
        + dma((2, NY - 1))
        + dma((2, 2, 2))
        + dma((NY + NZ + ndp - 3,))
        + dma((6,), 1)
        + dma((2, 2), 1),
        compiler_params=pltpu.CompilerParams(
            collective_id=0, has_side_effects=True, vmem_limit_bytes=62 << 20
        ),
    )(
        lengths,
        offsets,
        query_gain.reshape(1, D),
        key_gain.reshape(1, D),
        queries[0],
        out_grad[0],
        keys[0],
        values[0],
        pkeys[0],
        pvalues[0],
    )
    attention, query_grad, key_grad, value_grad, gains = pl.pallas_call(
        finish_kernel,
        name="finish",
        out_shape=[sd(x.shape, x.dtype) for x in results],
        in_specs=[ANY] * 5,
        out_specs=[HBM] * 5,
        scratch_shapes=[pltpu.VMEM(x.shape, x.dtype) for x in results] + [DMA((2, 11))],
        compiler_params=pltpu.CompilerParams(vmem_limit_bytes=62 << 20),
    )(*results)
    return attention[None], query_grad[None], key_grad[None], value_grad[None], gains


def solution(mesh):
    rows = P("dp", "context", None)
    in_specs = (rows,) * 6 + (P(), P(), P("dp", None), P("dp", None))
    out_specs = (rows,) * 4 + (P(),)
    return jax.shard_map(body, mesh=mesh, in_specs=in_specs, out_specs=out_specs, check_vma=False)
```
